32 devices in a mesh: dp: 8 (over z, y), tensor: 4 (over x, core).
Axes of the slice: x: 2, y: 2, z: 4, core: 2. Of those that a mesh axis runs over, the one named last changes fastest.
Arguments:
- acts: bfloat16 [8, 2048, 2048], P(None, 'dp', 'tensor'), may hold values from -24 to 24
- out_cot: bfloat16 [8, 2048, 1024], P(None, 'dp', 'tensor'), may hold values from -24 to 24
- emb_ids: int32 [2048], P(('dp', 'tensor')), may hold values from 0 to 8191
- emb_cot: bfloat16 [2048, 1024], P('dp', 'tensor'), may hold values from -24 to 24
- grad_w: float32 [8192, 2048], P(('dp', 'tensor')), may hold values from -6 to 6
- grad_e: float32 [8192, 1024], P(('dp', 'tensor')), may hold values from -6 to 6
Outputs:
- update_w: float32 [8192, 2048], P('dp', 'tensor')
- update_e: float32 [8192, 1024], P(('dp', 'tensor'))
The draws below stay inside these ranges and needn't reach their ends.
All inputs are finite; a program needn't handle non-finite values. Where the reference program divides by a largest or mean magnitude, that divisor is 1e-20 or more.
Results may differ from the reference program's by a relative error of at most 0.0003.
Values sent between devices are 32-bit elements; how exact they have to be, the bound alone decides.
No kernel may reach another device: no remote copies, remote signals or barrier semaphores. Data moves between devices by JAX's collectives and lax.ppermute only.
A program may use at most 64 MiB of HBM per device.

```python
import math
import jax
import jax.numpy as jnp
import numpy as np
from jax import lax

D = 1024
INNER = 2048
HEAD = 64
LAYERS = 8
NS_ITERS = 4
VOCAB = 8192
TOKENS = 2048


def scaled_rows(key, layers, cols):
    keys = jax.random.split(key, 4)
    shape = (layers, TOKENS, cols)
    groups = cols // HEAD
    rise = jnp.sqrt(1.0 + 2.0 * jnp.arange(TOKENS, dtype=jnp.float32) / TOKENS)
    base = jnp.clip(jax.random.normal(keys[0], shape, jnp.float32), -4.0, 4.0)
    common = 0.6 * jnp.clip(jax.random.normal(keys[1], (layers, TOKENS, groups), jnp.float32), -4.0, 4.0)
    row_scale = jnp.exp(jax.random.uniform(keys[2], (layers, TOKENS), jnp.float32, math.log(0.3), math.log(3.0)))
    col_scale = jnp.exp(jax.random.uniform(keys[3], (layers, cols), jnp.float32, math.log(0.3), math.log(3.0)))
    mixed = base + jnp.repeat(common, HEAD, axis=2)
    value = row_scale[:, :, None] * rise[None, :, None] * col_scale[:, None, :] * mixed
    return jnp.clip(value, -24.0, 24.0)


def draw_acts(key, part):
    return scaled_rows(jax.random.fold_in(key, 11), LAYERS, INNER).astype(jnp.bfloat16)


def draw_out_cot(key, part):
    return scaled_rows(jax.random.fold_in(key, 12), LAYERS, D).astype(jnp.bfloat16)


def draw_emb_cot(key, part):
    return scaled_rows(jax.random.fold_in(key, 13), 1, D)[0].astype(jnp.bfloat16)


def with_ends(drawn, stream_key, low, largest):
    extent = drawn.shape
    spot = [jax.random.randint(jax.random.fold_in(stream_key, axis), (), 0, extent[axis]) for axis in range(len(extent))]
    drawn = drawn.at[tuple(spot)].set(low)
    longest = extent.index(max(extent))
    spot[longest] = (spot[longest] + 1) % extent[longest]
    return drawn.at[tuple(spot)].set(largest)


def block_levels(own_key, dims, cuts, low, top_value):
    def one(position, blocks):
        heights = jax.random.uniform(jax.random.fold_in(jax.random.fold_in(own_key, 6), position), (blocks,), jnp.float32, low / len(cuts), top_value / len(cuts))
        return jnp.repeat(jnp.exp(heights), dims[position] // blocks).reshape((-1,) + (1,) * (len(dims) - position - 1))

    level = one(*cuts[0])
    for cut in cuts[1:]:
        level = level * one(*cut)
    return level


def rank_bounds(count, lean):
    loads = [(1 << 20) // math.isqrt(rank ** lean) + 1 for rank in range(1, count + 1)]
    scale = 1 + sum(loads) // (1 << 30)
    return np.cumsum(np.array([max(1, weight // scale) for weight in loads]))


def ranked_ids(stream_key, extent, count, lean):
    listing = rank_bounds(count, lean)
    ticket = jax.random.randint(jax.random.fold_in(stream_key, 1), extent, 0, int(listing[count - 1]))
    grade = jnp.searchsorted(jnp.asarray(listing, jnp.int32), ticket, side="right")
    return jax.random.permutation(jax.random.fold_in(stream_key, 2), count)[grade].astype(jnp.int32)


def noise(stream_key, shape, width, most, cuts=(), held_as=jnp.bfloat16):
    level = block_levels(stream_key, shape, cuts, -0.22, 0.18) if cuts else 1.0
    array = jax.random.normal(stream_key, shape, jnp.float32) * width * level
    return jnp.minimum(jnp.maximum(array, -most), most).astype(held_as)


def setup_inputs(seed: int = 0) -> dict:
    arg_keys = jax.random.split(jax.random.key(seed), 7)
    acts = draw_acts(jax.random.fold_in(arg_keys[6], 71), 0)
    out_cot = draw_out_cot(jax.random.fold_in(arg_keys[6], 71), 0)
    emb_ids = with_ends(ranked_ids(arg_keys[2], (TOKENS,), VOCAB, 2), jax.random.fold_in(arg_keys[2], 3), 0, VOCAB - 1).astype(jnp.int32)
    emb_cot = draw_emb_cot(jax.random.fold_in(arg_keys[6], 71), 0)
    grad_w = noise(arg_keys[4], (LAYERS * D, INNER), 1.0, 6.0, ((0, 32),), jnp.float32)
    grad_e = noise(arg_keys[5], (VOCAB, D), 1.0, 6.0, ((0, 32),), jnp.float32)
    return dict(acts=acts, out_cot=out_cot, emb_ids=emb_ids, emb_cot=emb_cot, grad_w=grad_w, grad_e=grad_e)


damp_root = 0.7

def newton_inverse(matrices):
    size = matrices.shape[-1]
    eye = jnp.eye(size, dtype=jnp.float32)
    bound = lax.optimization_barrier(jnp.max(lax.optimization_barrier(jnp.sum(jnp.abs(matrices), axis=-1)), axis=-1))
    approx = eye[None] / bound[:, None, None]
    for sweep in range(NS_ITERS):
        image = jnp.einsum('bij,bjk->bik', matrices, approx, precision=lax.Precision.HIGHEST)
        approx = jnp.einsum('bij,bjk->bik', approx, 2.0 * eye[None] - image, precision=lax.Precision.HIGHEST)
    return approx

def reference(acts, out_cot, emb_ids, emb_cot, grad_w, grad_e):
    heads = INNER // HEAD
    groups = D // HEAD

    def layer_grams(pair):
        inputs, grads = pair
        split_in = inputs.astype(jnp.float32).reshape(TOKENS, heads, HEAD)
        split_gr = grads.astype(jnp.float32).reshape(TOKENS, groups, HEAD)
        first = jnp.einsum('thi,thj->hij', split_in, split_in, precision=lax.Precision.HIGHEST)
        second = jnp.einsum('thi,thj->hij', split_gr, split_gr, precision=lax.Precision.HIGHEST)
        return (first, second)
    gram_a, gram_g = lax.map(layer_grams, (acts, out_cot))
    split_emb = emb_cot.astype(jnp.float32).reshape(TOKENS, groups, HEAD)
    gram_e = jnp.einsum('thi,thj->hij', split_emb, split_emb, precision=lax.Precision.HIGHEST)
    trace_a = lax.optimization_barrier(jnp.sum(jnp.trace(gram_a, axis1=2, axis2=3), axis=1))
    trace_g = lax.optimization_barrier(jnp.sum(jnp.trace(gram_g, axis1=2, axis2=3), axis=1))
    trace_e = jnp.sum(jnp.trace(gram_e, axis1=1, axis2=2))
    counts = jnp.zeros((VOCAB,), jnp.float32).at[emb_ids].add(1.0)
    ratio = jnp.sqrt(trace_a / (TOKENS * INNER) / (trace_g / (TOKENS * D)))
    ratio_e = jnp.sqrt(TOKENS / VOCAB / (trace_e / (TOKENS * D)))
    eye = jnp.eye(HEAD, dtype=jnp.float32)
    fac_a = gram_a / TOKENS + (damp_root * ratio)[:, None, None, None] * eye
    fac_g = gram_g / TOKENS + (damp_root / ratio)[:, None, None, None] * eye
    fac_e = gram_e / TOKENS + damp_root / ratio_e * eye
    row_scale = counts + damp_root * ratio_e
    inv_a = newton_inverse(fac_a.reshape(-1, HEAD, HEAD)).reshape(LAYERS, heads, HEAD, HEAD)
    inv_g = newton_inverse(fac_g.reshape(-1, HEAD, HEAD)).reshape(LAYERS, groups, HEAD, HEAD)
    inv_e = newton_inverse(fac_e)
    grad_view = grad_w.reshape(LAYERS, groups, HEAD, heads, HEAD)
    left = jnp.einsum('lgij,lgjhc->lgihc', inv_g, grad_view, precision=lax.Precision.HIGHEST)
    right = jnp.einsum('lgihc,lhcd->lgihd', left, inv_a, precision=lax.Precision.HIGHEST)
    update_w = right.reshape(LAYERS * D, INNER)
    scaled = jnp.einsum('rgi,gij->rgj', grad_e.reshape(VOCAB, groups, HEAD), inv_e, precision=lax.Precision.HIGHEST)
    update_e = scaled.reshape(VOCAB, D) / row_scale[:, None]
    return (update_w, update_e)
```

```python
import functools

import jax
import jax.numpy as jnp
from jax import lax
from jax.experimental import pallas as pl
from jax.experimental.pallas import tpu as pltpu
from jax.sharding import PartitionSpec as P

HEAD = 64
NS_ITERS = 4
LANES = 128
HALF = HEAD
ROWS = 8


damp_root = 0.7


def newton_inverse(matrices):
    size = matrices.shape[-1]
    eye = jnp.eye(size, dtype=jnp.float32)
    bound = jnp.max(jnp.sum(jnp.abs(matrices), axis=-1), axis=-1)
    approx = eye[None] / bound[:, None, None]
    for sweep in range(NS_ITERS):
        image = jnp.einsum("bij,bjk->bik", matrices, approx, precision=lax.Precision.HIGHEST)
        approx = jnp.einsum(
            "bij,bjk->bik", approx, 2.0 * eye[None] - image, precision=lax.Precision.HIGHEST
        )
    return approx


def general_local(acts, out_cot, emb_ids, emb_cot, grad_w, grad_e):
    n_dp = lax.axis_size("dp")
    n_tp = lax.axis_size("tensor")
    layers, tok_rows, inner_part = acts.shape
    width_part = out_cot.shape[2]
    heads_part = inner_part // HEAD
    groups_part = width_part // HEAD
    tokens_all = tok_rows * n_dp
    width = width_part * n_tp
    inner = inner_part * n_tp
    groups_all = width // HEAD
    rows_e = grad_e.shape[0]
    vocab = rows_e * n_dp * n_tp
    dp_index = lax.axis_index("dp")
    flat_index = dp_index * n_tp + lax.axis_index("tensor")
    tile_rows = grad_w.shape[0] * n_tp
    block_rows = tile_rows // HEAD
    layer_rows = min(tile_rows, width)
    layer_span = tile_rows // layer_rows
    first_layer = dp_index * tile_rows // width
    split_acts = acts.reshape(layers, tok_rows, heads_part, HEAD)
    gram_a = jnp.einsum(
        "lthi,lthj->lhij", split_acts, split_acts, preferred_element_type=jnp.float32
    )
    split_cot = out_cot.reshape(layers, tok_rows, groups_part, HEAD)
    gram_g = jnp.einsum("lthi,lthj->lhij", split_cot, split_cot, preferred_element_type=jnp.float32)
    split_emb = emb_cot.reshape(tok_rows, groups_part, HEAD)
    gram_e = jnp.einsum("thi,thj->hij", split_emb, split_emb, preferred_element_type=jnp.float32)
    blocks = jnp.concatenate(
        [gram_a.reshape(-1, HEAD, HEAD), gram_g.reshape(-1, HEAD, HEAD), gram_e], axis=0
    )
    block_count = blocks.shape[0]
    diagonal_sums = jnp.trace(blocks, axis1=1, axis2=2)
    local_a = jnp.sum(diagonal_sums[: layers * heads_part].reshape(layers, heads_part), axis=1)
    local_g = jnp.sum(
        diagonal_sums[layers * heads_part : layers * (heads_part + groups_part)].reshape(
            layers, groups_part
        ),
        axis=1,
    )
    local_e = jnp.sum(diagonal_sums[layers * (heads_part + groups_part) :])
    trace_local = jnp.concatenate([local_a, local_g, local_e[None]])
    local_counts = jnp.sum(
        (emb_ids[:, None] == jnp.arange(vocab, dtype=jnp.int32)[None, :]).astype(jnp.float32),
        axis=0,
    )
    traces, counts_all = lax.psum((trace_local, local_counts), ("dp", "tensor"))
    counts_mine = lax.dynamic_slice_in_dim(counts_all, flat_index * rows_e, rows_e)
    trace_a = traces[:layers]
    trace_g = traces[layers : 2 * layers]
    trace_e = traces[2 * layers]
    ratio = jnp.sqrt(trace_a / (tokens_all * inner) / (trace_g / (tokens_all * width)))
    ratio_e = jnp.sqrt(tokens_all / vocab / (trace_e / (tokens_all * width)))
    shift = jnp.concatenate(
        [
            jnp.repeat(damp_root * ratio, heads_part),
            jnp.repeat(damp_root / ratio, groups_part),
            jnp.full((groups_part,), 1.0, jnp.float32) * (damp_root / ratio_e),
        ]
    )
    eye = jnp.eye(HEAD, dtype=jnp.float32)
    owned = -(-block_count // n_dp)
    slots = owned * n_dp
    padded = jnp.pad(blocks.reshape(block_count, HEAD * HEAD), ((0, slots - block_count), (0, 0)))
    mine = lax.psum_scatter(padded, "dp", scatter_dimension=0, tiled=True)
    shift_pad = jnp.pad(shift, (0, slots - block_count), constant_values=1.0)
    shift_mine = lax.dynamic_slice_in_dim(shift_pad, dp_index * owned, owned)
    damped = mine.reshape(owned, HEAD, HEAD) / tokens_all + shift_mine[:, None, None] * eye
    inverse_mine = newton_inverse(damped)
    gathered = lax.all_gather(inverse_mine.reshape(owned, HEAD * HEAD), "dp", axis=0, tiled=True)
    inverses = gathered[:block_count].reshape(block_count, HEAD, HEAD)
    inv_a = inverses[: layers * heads_part].reshape(layers, heads_part, HEAD, HEAD)
    inv_g_part = inverses[layers * heads_part : layers * (heads_part + groups_part)].reshape(
        layers, groups_part, HEAD * HEAD
    )
    inv_e_part = inverses[layers * (heads_part + groups_part) :].reshape(groups_part, HEAD * HEAD)
    base_layer = 0
    sending = jnp.concatenate(
        [inv_g_part.reshape(layers * groups_part, HEAD * HEAD), inv_e_part], axis=0
    )
    shared = lax.all_gather(sending[None], "tensor", axis=0, tiled=True)
    inv_g = shared[:, : layers * groups_part].reshape(n_tp, layers, groups_part, HEAD, HEAD)
    inv_g = jnp.transpose(inv_g, (1, 0, 2, 3, 4)).reshape(layers * groups_all, HEAD, HEAD)
    inv_e = shared[:, layers * groups_part :].reshape(groups_all, HEAD, HEAD)
    tile = lax.all_to_all(grad_w, "tensor", split_axis=1, concat_axis=0, tiled=True)
    g_sel = lax.dynamic_slice_in_dim(
        inv_g, dp_index * block_rows - base_layer * groups_all, block_rows, 0
    )
    left = jnp.einsum(
        "bij,bjc->bic",
        g_sel,
        tile.reshape(block_rows, HEAD, inner_part),
        precision=lax.Precision.HIGHEST,
    )
    a_sel = lax.dynamic_slice_in_dim(inv_a, first_layer, layer_span, 0)
    right = jnp.einsum(
        "lrhi,lhij->lrhj",
        left.reshape(layer_span, layer_rows, heads_part, HEAD),
        a_sel,
        precision=lax.Precision.HIGHEST,
    )
    update_w = right.reshape(tile_rows, inner_part)
    scaled = jnp.einsum(
        "rgi,gij->rgj",
        grad_e.reshape(rows_e, groups_all, HEAD),
        inv_e,
        precision=lax.Precision.HIGHEST,
    )
    update_e = scaled.reshape(rows_e, width) / (counts_mine + damp_root * ratio_e)[:, None]
    return (update_w, update_e)


def pair_masks():
    row = lax.broadcasted_iota(jnp.int32, (HEAD, LANES), 0)
    lane = lax.broadcasted_iota(jnp.int32, (HEAD, LANES), 1)
    col = jnp.where(lane < HALF, lane, lane - HALF)
    return row, lane, col


def gram_pair(rows):
    full = lax.dot_general(
        rows, rows, (((0,), (0,)), ((), ())), preferred_element_type=jnp.float32
    )
    _, lane, _ = pair_masks()
    return jnp.where(lane < HALF, full[:HEAD], full[HEAD:])


def pack_quad(first, second):
    row, _, col = pair_masks()
    quad = jnp.where(col >= row, first, second)
    diagonal = jnp.sum(jnp.where(col == row, second, 0.0), axis=0, keepdims=True)
    return quad, diagonal


def unpack_quads(quad_a, diag_a, quad_b, diag_b):
    row, lane, col = pair_masks()
    turned = jnp.concatenate([quad_a, quad_b], axis=0).T
    top, low = turned[:HEAD], turned[HEAD:]
    turn_a = jnp.where(lane < HALF, top, pltpu.roll(low, HALF, 1))
    turn_b = jnp.where(lane < HALF, pltpu.roll(top, HALF, 1), low)

    def both(quad, turn, diag):
        first = jnp.where(col >= row, quad, turn)
        second = jnp.where(col < row, quad, jnp.where(col == row, diag, turn))
        return first, second

    return both(quad_a, turn_a, diag_a) + both(quad_b, turn_b, diag_b)


def split(value):
    high = value.astype(jnp.bfloat16)
    low = (value - high.astype(jnp.float32)).astype(jnp.bfloat16)
    return high, low


def block_diagonal(pair):
    row = lax.broadcasted_iota(jnp.int32, (LANES, LANES), 0)
    lane = lax.broadcasted_iota(jnp.int32, (LANES, LANES), 1)
    double = jnp.concatenate([pair, pair], axis=0)
    return jnp.where((row < HALF) == (lane < HALF), double, 0.0)


def right_factor(pair):
    high, low = split(block_diagonal(pair))
    wide = jnp.concatenate([high, low], axis=1)
    return jnp.concatenate([wide, wide], axis=0)


def times_right(value, factor):
    high, low = split(value)
    both = jnp.dot(
        jnp.concatenate([high, low], axis=1), factor, preferred_element_type=jnp.float32
    )
    return both[:, :LANES] + both[:, LANES:]


def left_factor(pair):
    high, low = split(block_diagonal(pair))
    return jnp.concatenate(
        [jnp.concatenate([high, high], axis=1), jnp.concatenate([low, low], axis=1)], axis=0
    )


def times_left(factor, value):
    high, low = split(value)
    both = jnp.dot(
        factor, jnp.concatenate([high, low], axis=0), preferred_element_type=jnp.float32
    )
    return both[:LANES] + both[LANES:]


def gram_kernel(quads_a, quads_g, me_ref, acts_ref, cot_ref, emb_ref, ids_ref, *refs):
    outs, emb_rows = refs[:-1], refs[-1]
    step = pl.program_id(0)
    quads = quads_a + 2 * quads_g
    diag_at = quads * HEAD

    def pack(source, at):
        first = gram_pair(source[:, at * 2 * LANES : (at * 2 + 1) * LANES])
        second = gram_pair(source[:, (at * 2 + 1) * LANES : (at * 2 + 2) * LANES])
        return pack_quad(first, second)

    @pl.when(step == 0)
    def _():
        for q in range(quads_g):
            quad, diagonal = pack(emb_ref[...], q)
            emb_rows[q * HEAD : (q + 1) * HEAD, :] = quad
            emb_rows[quads_g * HEAD + q : quads_g * HEAD + q + 1, :] = diagonal

    acts = acts_ref[0]
    cot = cot_ref[0]
    packed = [pack(acts, q) for q in range(quads_a)] + [pack(cot, q) for q in range(quads_g)]
    packed += [
        (
            emb_rows[q * HEAD : (q + 1) * HEAD, :],
            emb_rows[quads_g * HEAD + q : quads_g * HEAD + q + 1, :],
        )
        for q in range(quads_g)
    ]
    for j, out in enumerate(outs):

        @pl.when(step == j)
        def _(out=out):
            for q, (quad, diagonal) in enumerate(packed):
                out[q * HEAD : (q + 1) * HEAD, :] = quad
                out[diag_at + q : diag_at + q + 1, :] = diagonal
            out[diag_at + quads : diag_at + quads + 1, :] = ids_ref[...]


def grams(acts, out_cot, emb_cot, ids_row, dp_index, n_dp, quads_a, quads_g, payload_rows):
    layers, rows, width_a = acts.shape
    width_g = out_cot.shape[2]
    emb_scratch = -(-(quads_g * HEAD + quads_g) // ROWS) * ROWS
    spec = pltpu.PrefetchScalarGridSpec(
        num_scalar_prefetch=1,
        grid=(n_dp,),
        in_specs=[
            pl.BlockSpec((1, rows, width_a), lambda k, me: (lax.bitwise_xor(me[0], k), 0, 0)),
            pl.BlockSpec((1, rows, width_g), lambda k, me: (lax.bitwise_xor(me[0], k), 0, 0)),
            pl.BlockSpec((rows, width_g), lambda k, me: (0, 0)),
            pl.BlockSpec((1, LANES), lambda k, me: (0, 0)),
        ],
        out_specs=[pl.BlockSpec((payload_rows, LANES), lambda k, me: (0, 0))] * n_dp,
        scratch_shapes=[pltpu.VMEM((emb_scratch, LANES), jnp.float32)],
    )
    return pl.pallas_call(
        functools.partial(gram_kernel, quads_a, quads_g),
        grid_spec=spec,
        out_shape=[jax.ShapeDtypeStruct((payload_rows, LANES), jnp.float32)] * n_dp,
        cost_estimate=pl.CostEstimate(flops=1000, bytes_accessed=1000, transcendentals=0),
        name="grams",
    )(dp_index.reshape(1), acts, out_cot, emb_cot, ids_row)


def sum_kernel(quads_a, quads_g, *refs):
    n_dp = len(refs) - 2
    parts, (own_ref, share_ref) = refs[:n_dp], refs[n_dp:]
    quads = quads_a + 2 * quads_g
    diag_at = quads * HEAD

    def total(at, size):
        value = parts[0][at : at + size, :]
        for part in parts[1:]:
            value = value + part[at : at + size, :]
        return value

    row, _, col = pair_masks()
    traces = []
    first = 0
    for count, where in ((quads_a, own_ref), (quads_g, share_ref), (quads_g, share_ref)):
        trace = jnp.zeros((1, LANES), jnp.float32)
        for q in range(first, first + count):
            quad = total(q * HEAD, HEAD)
            diagonal = total(diag_at + q, 1)
            trace = trace + diagonal
            trace = trace + jnp.sum(jnp.where(col == row, quad, 0.0), axis=0, keepdims=True)
            if where is own_ref:
                own_ref[q * HEAD : (q + 1) * HEAD, :] = quad
                own_ref[quads_a * HEAD + q : quads_a * HEAD + q + 1, :] = diagonal
            else:
                at = q - quads_a
                share_ref[at * HEAD : (at + 1) * HEAD, :] = quad
                share_ref[2 * quads_g * HEAD + at : 2 * quads_g * HEAD + at + 1, :] = diagonal
        traces.append(trace)
        first += count
    at = 2 * quads_g * (HEAD + 1)
    for trace in traces:
        share_ref[at : at + 1, :] = trace
        at += 1
    for part in parts:
        share_ref[at : at + 1, :] = part[diag_at + quads : diag_at + quads + 1, :]
        at += 1


def invert_apply_kernel(sizes, own_ref, share_ref, w_ref, e_ref, w_out, e_out, right_a, left_g, right_e, scale):
    quads_a, quads_g, n_tp, n_dp, tokens, vocab, inner, width = sizes
    step = pl.program_id(0)
    trace_at = 2 * quads_g * (HEAD + 1)

    @pl.when(step == 0)
    def _():
        def trace_of(kind):
            value = share_ref[0, trace_at + kind : trace_at + kind + 1, :]
            for t in range(1, n_tp):
                value = value + share_ref[t, trace_at + kind : trace_at + kind + 1, :]
            return jnp.sum(value, axis=1, keepdims=True)

        trace_a, trace_g, trace_e = trace_of(0), trace_of(1), trace_of(2)
        ratio = jnp.sqrt(trace_a / (tokens * inner) / (trace_g / (tokens * width)))
        ratio_e = jnp.sqrt(tokens / vocab / (trace_e / (tokens * width)))

        rows_e = scale.shape[0]
        base = (
            (lax.axis_index("dp") * n_tp + lax.axis_index("tensor")) * rows_e
        ).astype(jnp.float32)
        index = lax.broadcasted_iota(jnp.int32, (rows_e, LANES), 0).astype(jnp.float32) + base
        hits = jnp.zeros((rows_e, LANES), jnp.float32)
        for t in range(n_tp):
            for d in range(n_dp):
                ids = share_ref[t, trace_at + 3 + d : trace_at + 4 + d, :]
                hits = hits + jnp.where(index == ids, 1.0, 0.0)
        counts = jnp.sum(hits, axis=1, keepdims=True)
        scale[...] = jnp.broadcast_to(
            1.0 / (counts + damp_root * ratio_e), (rows_e, LANES)
        )

        packed = []
        for q in range(quads_a):
            packed.append((own_ref, (), q, quads_a * HEAD + q))
        for kind in range(2):
            for t in range(n_tp):
                for q in range(kind * quads_g, (kind + 1) * quads_g):
                    packed.append((share_ref, (t,), q, 2 * quads_g * HEAD + q))
        loaded = [
            (
                ref[(*lead, slice(q * HEAD, (q + 1) * HEAD), slice(None))],
                ref[(*lead, slice(d, d + 1), slice(None))],
            )
            for ref, lead, q, d in packed
        ]
        pairs = []
        for i in range(0, len(loaded), 2):
            pairs += unpack_quads(*loaded[i], *loaded[i + 1])

        row, lane, col = pair_masks()
        eye = jnp.where(col == row, 1.0, 0.0)
        shifts = (
            [damp_root * ratio] * (2 * quads_a)
            + [damp_root / ratio] * (2 * quads_g * n_tp)
            + [damp_root / ratio_e] * (2 * quads_g * n_tp)
        )
        scaled, over = [], []
        for pair, shift in zip(pairs, shifts):
            damped = pair / tokens + shift * eye
            sums = jnp.sum(jnp.abs(damped), axis=0, keepdims=True)
            lane_row = lane[:1]
            bound = jnp.where(
                lane_row < HALF,
                jnp.max(jnp.where(lane_row < HALF, sums, 0.0), axis=1, keepdims=True),
                jnp.max(jnp.where(lane_row < HALF, 0.0, sums), axis=1, keepdims=True),
            )
            inverse_bound = 1.0 / bound
            scaled.append(damped * inverse_bound)
            over.append(inverse_bound)

        for i in range(len(pairs)):
            image = scaled[i]
            approx = 2.0 * eye - image
            image = 2.0 * image - times_right(image, right_factor(image))
            for sweep in range(1, NS_ITERS):
                factor = right_factor(image)
                if sweep < NS_ITERS - 1:
                    product = times_right(jnp.concatenate([approx, image], axis=0), factor)
                    approx = 2.0 * approx - product[:HEAD]
                    image = 2.0 * image - product[HEAD:]
                else:
                    approx = 2.0 * approx - times_right(approx, factor)
            inverse = approx * over[i]
            if i < 2 * quads_a:
                right_a[i] = right_factor(inverse)
            elif i < 2 * quads_a + 2 * quads_g * n_tp:
                left_g[i - 2 * quads_a] = left_factor(inverse)
            else:
                right_e[i - 2 * quads_a - 2 * quads_g * n_tp] = right_factor(inverse)

    left = times_left(left_g[step], w_ref[...])
    for h in range(2 * quads_a):
        at = slice(h * LANES, (h + 1) * LANES)
        w_out[:, at] = times_right(left[:, at], right_a[h])
    e_out[...] = times_right(e_ref[...], right_e[step]) * scale[...]


def local(acts, out_cot, emb_ids, emb_cot, grad_w, grad_e):
    n_dp = lax.axis_size("dp")
    n_tp = lax.axis_size("tensor")
    layers, tok_rows, inner_part = acts.shape
    width_part = out_cot.shape[2]
    width = width_part * n_tp
    rows_e = grad_e.shape[0]
    tile_rows = grad_w.shape[0] * n_tp
    direct = (
        layers == n_dp
        and n_dp & (n_dp - 1) == 0
        and tile_rows == width
        and inner_part % (2 * LANES) == 0
        and width_part % (2 * LANES) == 0
        and (inner_part // (2 * LANES)) % 2 == 0
        and n_tp % 2 == 0
        and emb_ids.shape[0] <= LANES
        and rows_e % ROWS == 0
    )
    if not direct:
        return general_local(acts, out_cot, emb_ids, emb_cot, grad_w, grad_e)
    quads_a = inner_part // (2 * LANES)
    quads_g = width_part // (2 * LANES)
    quads = quads_a + 2 * quads_g
    dp_index = lax.axis_index("dp")
    sending = grad_w.reshape(grad_w.shape[0], n_tp, inner_part).transpose(1, 0, 2)
    tile = lax.all_to_all(sending, "tensor", split_axis=0, concat_axis=0, tiled=True)
    tile = tile.reshape(tile_rows, inner_part)

    ids_row = jnp.pad(
        emb_ids.astype(jnp.float32), (0, LANES - emb_ids.shape[0]), constant_values=-1.0
    ).reshape(1, LANES)
    payload_rows = -(-(quads * (HEAD + 1) + 1) // ROWS) * ROWS
    parts = grams(
        acts, out_cot, emb_cot, ids_row, dp_index, n_dp, quads_a, quads_g, payload_rows
    )
    arrived = [parts[0]] + [
        lax.ppermute(parts[k], "dp", [(i, i ^ k) for i in range(n_dp)])
        for k in range(n_dp - 1, 0, -1)
    ]
    own_rows = -(-quads_a * (HEAD + 1) // ROWS) * ROWS
    share_rows = -(-(2 * quads_g * (HEAD + 1) + 3 + n_dp) // ROWS) * ROWS
    own, share = pl.pallas_call(
        functools.partial(sum_kernel, quads_a, quads_g),
        out_shape=[
            jax.ShapeDtypeStruct((own_rows, LANES), jnp.float32),
            jax.ShapeDtypeStruct((share_rows, LANES), jnp.float32),
        ],
        cost_estimate=pl.CostEstimate(flops=1000, bytes_accessed=1000, transcendentals=0),
        name="sums",
    )(*arrived)
    shared = lax.all_gather(share[None], "tensor", axis=0, tiled=True)

    steps = tile_rows // LANES
    sizes = (
        quads_a,
        quads_g,
        n_tp,
        n_dp,
        tok_rows * n_dp,
        rows_e * n_dp * n_tp,
        inner_part * n_tp,
        width,
    )
    return pl.pallas_call(
        functools.partial(invert_apply_kernel, sizes),
        grid=(steps,),
        in_specs=[
            pl.BlockSpec((own_rows, LANES), lambda i: (0, 0)),
            pl.BlockSpec((n_tp, share_rows, LANES), lambda i: (0, 0, 0)),
            pl.BlockSpec((LANES, inner_part), lambda i: (i, 0)),
            pl.BlockSpec((rows_e, LANES), lambda i: (0, i)),
        ],
        out_specs=[
            pl.BlockSpec((LANES, inner_part), lambda i: (i, 0)),
            pl.BlockSpec((rows_e, LANES), lambda i: (0, i)),
        ],
        out_shape=[
            jax.ShapeDtypeStruct((tile_rows, inner_part), jnp.float32),
            jax.ShapeDtypeStruct((rows_e, width), jnp.float32),
        ],
        scratch_shapes=[
            pltpu.VMEM((2 * quads_a, 2 * LANES, 2 * LANES), jnp.bfloat16),
            pltpu.VMEM((steps, 2 * LANES, 2 * LANES), jnp.bfloat16),
            pltpu.VMEM((steps, 2 * LANES, 2 * LANES), jnp.bfloat16),
            pltpu.VMEM((rows_e, LANES), jnp.float32),
        ],
        compiler_params=pltpu.CompilerParams(vmem_limit_bytes=32 * 1024 * 1024),
        cost_estimate=pl.CostEstimate(flops=1000, bytes_accessed=1000, transcendentals=0),
        name="invert_apply",
    )(own, shared, tile, grad_e)


def solution(mesh):
    in_specs = (
        P(None, "dp", "tensor"),
        P(None, "dp", "tensor"),
        P(("dp", "tensor")),
        P("dp", "tensor"),
        P(("dp", "tensor"), None),
        P(("dp", "tensor"), None),
    )
    out_specs = (P("dp", "tensor"), P(("dp", "tensor"), None))
    return jax.shard_map(local, mesh=mesh, in_specs=in_specs, out_specs=out_specs, check_vma=False)
```

```python
import functools

import jax
import jax.numpy as jnp
from jax import lax
from jax.experimental import pallas as pl
from jax.experimental.pallas import tpu as pltpu
from jax.sharding import PartitionSpec as P

HEAD = 64
NS_ITERS = 4
LANES = 128
HALF = HEAD
ROWS = 8


damp_root = 0.7


def newton_inverse(matrices):
    size = matrices.shape[-1]
    eye = jnp.eye(size, dtype=jnp.float32)
    bound = jnp.max(jnp.sum(jnp.abs(matrices), axis=-1), axis=-1)
    approx = eye[None] / bound[:, None, None]
    for sweep in range(NS_ITERS):
        image = jnp.einsum("bij,bjk->bik", matrices, approx, precision=lax.Precision.HIGHEST)
        approx = jnp.einsum(
            "bij,bjk->bik", approx, 2.0 * eye[None] - image, precision=lax.Precision.HIGHEST
        )
    return approx


def general_local(acts, out_cot, emb_ids, emb_cot, grad_w, grad_e):
    n_dp = lax.axis_size("dp")
    n_tp = lax.axis_size("tensor")
    layers, tok_rows, inner_part = acts.shape
    width_part = out_cot.shape[2]
    heads_part = inner_part // HEAD
    groups_part = width_part // HEAD
    tokens_all = tok_rows * n_dp
    width = width_part * n_tp
    inner = inner_part * n_tp
    groups_all = width // HEAD
    rows_e = grad_e.shape[0]
    vocab = rows_e * n_dp * n_tp
    dp_index = lax.axis_index("dp")
    flat_index = dp_index * n_tp + lax.axis_index("tensor")
    tile_rows = grad_w.shape[0] * n_tp
    block_rows = tile_rows // HEAD
    layer_rows = min(tile_rows, width)
    layer_span = tile_rows // layer_rows
    first_layer = dp_index * tile_rows // width
    split_acts = acts.reshape(layers, tok_rows, heads_part, HEAD)
    gram_a = jnp.einsum(
        "lthi,lthj->lhij", split_acts, split_acts, preferred_element_type=jnp.float32
    )
    split_cot = out_cot.reshape(layers, tok_rows, groups_part, HEAD)
    gram_g = jnp.einsum("lthi,lthj->lhij", split_cot, split_cot, preferred_element_type=jnp.float32)
    split_emb = emb_cot.reshape(tok_rows, groups_part, HEAD)
    gram_e = jnp.einsum("thi,thj->hij", split_emb, split_emb, preferred_element_type=jnp.float32)
    blocks = jnp.concatenate(
        [gram_a.reshape(-1, HEAD, HEAD), gram_g.reshape(-1, HEAD, HEAD), gram_e], axis=0
    )
    block_count = blocks.shape[0]
    diagonal_sums = jnp.trace(blocks, axis1=1, axis2=2)
    local_a = jnp.sum(diagonal_sums[: layers * heads_part].reshape(layers, heads_part), axis=1)
    local_g = jnp.sum(
        diagonal_sums[layers * heads_part : layers * (heads_part + groups_part)].reshape(
            layers, groups_part
        ),
        axis=1,
    )
    local_e = jnp.sum(diagonal_sums[layers * (heads_part + groups_part) :])
    trace_local = jnp.concatenate([local_a, local_g, local_e[None]])
    local_counts = jnp.sum(
        (emb_ids[:, None] == jnp.arange(vocab, dtype=jnp.int32)[None, :]).astype(jnp.float32),
        axis=0,
    )
    traces, counts_all = lax.psum((trace_local, local_counts), ("dp", "tensor"))
    counts_mine = lax.dynamic_slice_in_dim(counts_all, flat_index * rows_e, rows_e)
    trace_a = traces[:layers]
    trace_g = traces[layers : 2 * layers]
    trace_e = traces[2 * layers]
    ratio = jnp.sqrt(trace_a / (tokens_all * inner) / (trace_g / (tokens_all * width)))
    ratio_e = jnp.sqrt(tokens_all / vocab / (trace_e / (tokens_all * width)))
    shift = jnp.concatenate(
        [
            jnp.repeat(damp_root * ratio, heads_part),
            jnp.repeat(damp_root / ratio, groups_part),
            jnp.full((groups_part,), 1.0, jnp.float32) * (damp_root / ratio_e),
        ]
    )
    eye = jnp.eye(HEAD, dtype=jnp.float32)
    owned = -(-block_count // n_dp)
    slots = owned * n_dp
    padded = jnp.pad(blocks.reshape(block_count, HEAD * HEAD), ((0, slots - block_count), (0, 0)))
    mine = lax.psum_scatter(padded, "dp", scatter_dimension=0, tiled=True)
    shift_pad = jnp.pad(shift, (0, slots - block_count), constant_values=1.0)
    shift_mine = lax.dynamic_slice_in_dim(shift_pad, dp_index * owned, owned)
    damped = mine.reshape(owned, HEAD, HEAD) / tokens_all + shift_mine[:, None, None] * eye
    inverse_mine = newton_inverse(damped)
    gathered = lax.all_gather(inverse_mine.reshape(owned, HEAD * HEAD), "dp", axis=0, tiled=True)
    inverses = gathered[:block_count].reshape(block_count, HEAD, HEAD)
    inv_a = inverses[: layers * heads_part].reshape(layers, heads_part, HEAD, HEAD)
    inv_g_part = inverses[layers * heads_part : layers * (heads_part + groups_part)].reshape(
        layers, groups_part, HEAD * HEAD
    )
    inv_e_part = inverses[layers * (heads_part + groups_part) :].reshape(groups_part, HEAD * HEAD)
    base_layer = 0
    sending = jnp.concatenate(
        [inv_g_part.reshape(layers * groups_part, HEAD * HEAD), inv_e_part], axis=0
    )
    shared = lax.all_gather(sending[None], "tensor", axis=0, tiled=True)
    inv_g = shared[:, : layers * groups_part].reshape(n_tp, layers, groups_part, HEAD, HEAD)
    inv_g = jnp.transpose(inv_g, (1, 0, 2, 3, 4)).reshape(layers * groups_all, HEAD, HEAD)
    inv_e = shared[:, layers * groups_part :].reshape(groups_all, HEAD, HEAD)
    tile = lax.all_to_all(grad_w, "tensor", split_axis=1, concat_axis=0, tiled=True)
    g_sel = lax.dynamic_slice_in_dim(
        inv_g, dp_index * block_rows - base_layer * groups_all, block_rows, 0
    )
    left = jnp.einsum(
        "bij,bjc->bic",
        g_sel,
        tile.reshape(block_rows, HEAD, inner_part),
        precision=lax.Precision.HIGHEST,
    )
    a_sel = lax.dynamic_slice_in_dim(inv_a, first_layer, layer_span, 0)
    right = jnp.einsum(
        "lrhi,lhij->lrhj",
        left.reshape(layer_span, layer_rows, heads_part, HEAD),
        a_sel,
        precision=lax.Precision.HIGHEST,
    )
    update_w = right.reshape(tile_rows, inner_part)
    scaled = jnp.einsum(
        "rgi,gij->rgj",
        grad_e.reshape(rows_e, groups_all, HEAD),
        inv_e,
        precision=lax.Precision.HIGHEST,
    )
    update_e = scaled.reshape(rows_e, width) / (counts_mine + damp_root * ratio_e)[:, None]
    return (update_w, update_e)


def pair_masks():
    row = lax.broadcasted_iota(jnp.int32, (HEAD, LANES), 0)
    lane = lax.broadcasted_iota(jnp.int32, (HEAD, LANES), 1)
    col = jnp.where(lane < HALF, lane, lane - HALF)
    return row, lane, col


def gram_pair(rows):
    full = lax.dot_general(
        rows, rows, (((0,), (0,)), ((), ())), preferred_element_type=jnp.float32
    )
    _, lane, _ = pair_masks()
    return jnp.where(lane < HALF, full[:HEAD], full[HEAD:])


def pack_quad(first, second):
    row, _, col = pair_masks()
    quad = jnp.where(col >= row, first, second)
    diagonal = jnp.sum(jnp.where(col == row, second, 0.0), axis=0, keepdims=True)
    return quad, diagonal


def unpack_quads(quad_a, diag_a, quad_b, diag_b):
    row, lane, col = pair_masks()
    turned = jnp.concatenate([quad_a, quad_b], axis=0).T
    top, low = turned[:HEAD], turned[HEAD:]
    turn_a = jnp.where(lane < HALF, top, pltpu.roll(low, HALF, 1))
    turn_b = jnp.where(lane < HALF, pltpu.roll(top, HALF, 1), low)

    def both(quad, turn, diag):
        first = jnp.where(col >= row, quad, turn)
        second = jnp.where(col < row, quad, jnp.where(col == row, diag, turn))
        return first, second

    return both(quad_a, turn_a, diag_a) + both(quad_b, turn_b, diag_b)


def split(value):
    high = value.astype(jnp.bfloat16)
    low = (value - high.astype(jnp.float32)).astype(jnp.bfloat16)
    return high, low


def block_diagonal(pair):
    row = lax.broadcasted_iota(jnp.int32, (LANES, LANES), 0)
    lane = lax.broadcasted_iota(jnp.int32, (LANES, LANES), 1)
    double = jnp.concatenate([pair, pair], axis=0)
    return jnp.where((row < HALF) == (lane < HALF), double, jnp.zeros_like(double))


def blocks_right(high, low):
    wide = jnp.concatenate([block_diagonal(high), block_diagonal(low)], axis=1)
    return jnp.concatenate([wide, wide], axis=0)


def blocks_left(high, low):
    high, low = block_diagonal(high), block_diagonal(low)
    return jnp.concatenate(
        [jnp.concatenate([high, high], axis=1), jnp.concatenate([low, low], axis=1)], axis=0
    )


def add_halves(both):
    return both[:, :LANES] + both[:, LANES:]


def split_times(parts, factor):
    return add_halves(
        jnp.dot(jnp.concatenate(parts, axis=1), factor, preferred_element_type=jnp.float32)
    )


def gram_kernel(counts, me_ref, ids_ref, acts_hbm, cot_hbm, emb_hbm, w_hbm, *refs):
    quads_a, quads_g, n_dp, n_tp = counts
    half = n_dp // 2
    outs, w_out = refs[:half], refs[half]
    acts, cot, emb, acts_sem, cot_sem, emb_sem, w_sem = refs[half + 1 :]
    me = me_ref[0]
    order = [k for j in list(range(1, half)) + [0] for k in (j, j + half)]

    def fetch(k):
        layer = lax.bitwise_xor(me, k)
        return (
            pltpu.make_async_copy(acts_hbm.at[layer], acts.at[k], acts_sem.at[k]),
            pltpu.make_async_copy(cot_hbm.at[layer], cot.at[k], cot_sem.at[k]),
        )

    emb_copy = pltpu.make_async_copy(emb_hbm, emb, emb_sem)
    emb_copy.start()
    for k in order:
        for copy in fetch(k):
            copy.start()
    part = w_hbm.shape[1] // n_tp
    moves = [
        pltpu.make_async_copy(w_hbm.at[:, pl.ds(t * part, part)], w_out.at[t], w_sem.at[t])
        for t in range(n_tp)
    ]
    for move in moves:
        move.start()

    def pack(source, at):
        first = gram_pair(source[:, at * 2 * LANES : (at * 2 + 1) * LANES])
        second = gram_pair(source[:, (at * 2 + 1) * LANES : (at * 2 + 2) * LANES])
        return pack_quad(first, second)

    emb_copy.wait()
    emb_rows = emb[...]
    packed_e = [pack(emb_rows, q) for q in range(quads_g)]
    ids = jnp.concatenate(
        [
            ids_ref[...].astype(jnp.float32),
            jnp.full((1, LANES - ids_ref.shape[1]), -1.0, jnp.float32),
        ],
        axis=1,
    )
    for j in list(range(1, half)) + [0]:
        packed = []
        for k in (j, j + half):
            for copy in fetch(k):
                copy.wait()
            rows_a, rows_g = acts[k], cot[k]
            packed += [pack(rows_a, q) for q in range(quads_a)]
            packed += [pack(rows_g, q) for q in range(quads_g)]
        packed += packed_e
        for q, (quad, diagonal) in enumerate(packed):
            outs[j][q * HEAD : (q + 1) * HEAD, :] = quad
            at = len(packed) * HEAD + q
            outs[j][at : at + 1, :] = diagonal
        at = len(packed) * (HEAD + 1)
        outs[j][at : at + 1, :] = ids
    for move in moves:
        move.wait()


def small_cost():
    return pl.CostEstimate(flops=1000, bytes_accessed=1000, transcendentals=0)


def round_up(value, unit):
    return -(-value // unit) * unit


def grams(acts, out_cot, emb_cot, emb_ids, grad_w, dp_index, n_dp, n_tp, quads_a, quads_g):
    layers, rows, width_a = acts.shape
    width_g = out_cot.shape[2]
    half = n_dp // 2
    payload_rows = round_up((2 * (quads_a + quads_g) + quads_g) * (HEAD + 1) + 1, ROWS)
    part = grad_w.shape[1] // n_tp
    vmem = pl.BlockSpec(memory_space=pltpu.VMEM)
    hbm = pl.BlockSpec(memory_space=pltpu.HBM)
    return pl.pallas_call(
        functools.partial(gram_kernel, (quads_a, quads_g, n_dp, n_tp)),
        in_specs=[pl.BlockSpec(memory_space=pltpu.SMEM), vmem, hbm, hbm, hbm, hbm],
        out_specs=[vmem] * half + [hbm],
        out_shape=[jax.ShapeDtypeStruct((payload_rows, LANES), jnp.float32)] * half
        + [jax.ShapeDtypeStruct((n_tp, grad_w.shape[0], part), jnp.float32)],
        scratch_shapes=[
            pltpu.VMEM((layers, rows, width_a), jnp.bfloat16),
            pltpu.VMEM((layers, rows, width_g), jnp.bfloat16),
            pltpu.VMEM((rows, width_g), jnp.bfloat16),
            pltpu.SemaphoreType.DMA((layers,)),
            pltpu.SemaphoreType.DMA((layers,)),
            pltpu.SemaphoreType.DMA,
            pltpu.SemaphoreType.DMA((n_tp,)),
        ],
        compiler_params=pltpu.CompilerParams(vmem_limit_bytes=32 * 1024 * 1024),
        cost_estimate=small_cost(),
        name="grams",
    )(dp_index.reshape(1), emb_ids.reshape(1, -1), acts, out_cot, emb_cot, grad_w)


def half_sum_kernel(quads_layer, quads_g, *refs):
    parts, outs = refs[:-2], refs[-2:]
    quads_in = 2 * quads_layer + quads_g
    quads_out = quads_layer + quads_g

    def total(at, size):
        value = parts[0][at : at + size, :]
        for part in parts[1:]:
            value = value + part[at : at + size, :]
        return value

    shared = [
        (total(q * HEAD, HEAD), total(quads_in * HEAD + q, 1))
        for q in range(2 * quads_layer, quads_in)
    ]
    for place, out in enumerate(outs):
        both = [
            (total(q * HEAD, HEAD), total(quads_in * HEAD + q, 1))
            for q in range(place * quads_layer, (place + 1) * quads_layer)
        ]
        for q, (quad, diagonal) in enumerate(both + shared):
            out[q * HEAD : (q + 1) * HEAD, :] = quad
            out[quads_out * HEAD + q : quads_out * HEAD + q + 1, :] = diagonal
        at = quads_out * (HEAD + 1)
        for i, part in enumerate(parts):
            ids_at = quads_in * (HEAD + 1)
            out[at + i : at + i + 1, :] = part[ids_at : ids_at + 1, :]


def sum_kernel(quads_a, quads_g, half, kept, came, own_ref, share_ref):
    quads = quads_a + 2 * quads_g
    diag_at = quads * HEAD
    row, _, col = pair_masks()
    traces = []
    first = 0
    for count, where in ((quads_a, own_ref), (quads_g, share_ref), (quads_g, share_ref)):
        trace = jnp.zeros((1, LANES), jnp.float32)
        for q in range(first, first + count):
            at = slice(q * HEAD, (q + 1) * HEAD)
            quad = kept[at, :] + came[at, :]
            at = slice(diag_at + q, diag_at + q + 1)
            diagonal = kept[at, :] + came[at, :]
            trace = trace + diagonal
            trace = trace + jnp.sum(jnp.where(col == row, quad, 0.0), axis=0, keepdims=True)
            if where is own_ref:
                own_ref[q * HEAD : (q + 1) * HEAD, :] = quad
                own_ref[quads_a * HEAD + q : quads_a * HEAD + q + 1, :] = diagonal
            else:
                at = q - quads_a
                share_ref[at * HEAD : (at + 1) * HEAD, :] = quad
                share_ref[2 * quads_g * HEAD + at : 2 * quads_g * HEAD + at + 1, :] = diagonal
        traces.append(trace)
        first += count
    at = 2 * quads_g * (HEAD + 1)
    for trace in traces:
        share_ref[at : at + 1, :] = trace
        at += 1
    for ref in (kept, came):
        for i in range(half):
            ids_at = quads * (HEAD + 1) + i
            share_ref[at : at + 1, :] = ref[ids_at : ids_at + 1, :]
            at += 1


def invert_apply_kernel(sizes, own_ref, share_hbm, w_hbm, e_hbm, w_out, e_out, *scratch):
    quads_a, quads_g, n_tp, n_dp, tokens, vocab, inner, width, chunk = sizes
    share, w_in, e_in, w_done, e_done, share_sem, w_sem, e_sem, w_out_sem, e_out_sem = scratch
    tile_rows, inner_part = w_in.shape
    rows_e = e_in.shape[0]
    chunks = tile_rows // chunk
    e_parts = 2
    e_cols = width // e_parts
    share_copy = pltpu.make_async_copy(share_hbm, share, share_sem)
    w_loads = [
        pltpu.make_async_copy(
            w_hbm.at[pl.ds(c * chunk, chunk)], w_in.at[pl.ds(c * chunk, chunk)], w_sem.at[c]
        )
        for c in range(chunks)
    ]
    e_load = pltpu.make_async_copy(e_hbm, e_in, e_sem)
    share_copy.start()
    e_load.start()
    for load in w_loads:
        load.start()
    share_copy.wait()

    trace_at = 2 * quads_g * (HEAD + 1)

    def trace_of(kind):
        value = share[0, trace_at + kind : trace_at + kind + 1, :]
        for t in range(1, n_tp):
            value = value + share[t, trace_at + kind : trace_at + kind + 1, :]
        return jnp.sum(value, axis=1, keepdims=True)

    trace_a, trace_g, trace_e = trace_of(0), trace_of(1), trace_of(2)
    ratio = jnp.sqrt(trace_a / (tokens * inner) / (trace_g / (tokens * width)))
    ratio_e = jnp.sqrt(tokens / vocab / (trace_e / (tokens * width)))

    loaded = [
        (
            own_ref[q * HEAD : (q + 1) * HEAD, :],
            own_ref[quads_a * HEAD + q : quads_a * HEAD + q + 1, :],
        )
        for q in range(quads_a)
    ]
    diag_at = 2 * quads_g * HEAD
    for kind in range(2):
        for t in range(n_tp):
            for q in range(kind * quads_g, (kind + 1) * quads_g):
                loaded.append(
                    (
                        share[t, q * HEAD : (q + 1) * HEAD, :],
                        share[t, diag_at + q : diag_at + q + 1, :],
                    )
                )
    pairs = []
    for i in range(0, len(loaded), 2):
        pairs += unpack_quads(*loaded[i], *loaded[i + 1])
    n_a, n_g = 2 * quads_a, 2 * quads_g * n_tp

    row, lane, col = pair_masks()
    eye = jnp.where(col == row, 1.0, 0.0)
    low_lane = lane[:1] < HALF
    shifts = [damp_root * ratio] * n_a + [damp_root / ratio] * n_g + [damp_root / ratio_e] * n_g
    images, over = [], []
    for pair, shift in zip(pairs, shifts):
        damped = pair * (1.0 / tokens) + shift * eye
        sums = jnp.sum(jnp.abs(damped), axis=0, keepdims=True)
        bound = jnp.where(
            low_lane,
            jnp.max(jnp.where(low_lane, sums, 0.0), axis=1, keepdims=True),
            jnp.max(jnp.where(low_lane, 0.0, sums), axis=1, keepdims=True),
        )
        inverse_bound = 1.0 / bound
        images.append(damped * inverse_bound)
        over.append(inverse_bound)
    approx = [2.0 * eye - image for image in images]
    for sweep in range(NS_ITERS):
        splits = [split(image) for image in images]
        factors = [blocks_right(*parts) for parts in splits]
        if sweep == 0:
            images = [
                2.0 * image - split_times(parts, factor)
                for image, parts, factor in zip(images, splits, factors)
            ]
        elif sweep < NS_ITERS - 1:
            products = []
            for value, parts, factor in zip(approx, splits, factors):
                stacked = [
                    jnp.concatenate([a, b], axis=0) for a, b in zip(split(value), parts)
                ]
                products.append(split_times(stacked, factor))
            approx = [2.0 * a - p[:HEAD] for a, p in zip(approx, products)]
            images = [2.0 * b - p[HEAD:] for b, p in zip(images, products)]
        else:
            approx = [
                2.0 * a - split_times(split(a), factor) for a, factor in zip(approx, factors)
            ]
    inverses = [split(a * b) for a, b in zip(approx, over)]
    right_a = [blocks_right(*parts) for parts in inverses[:n_a]]

    base = ((lax.axis_index("dp") * n_tp + lax.axis_index("tensor")) * rows_e).astype(jnp.float32)
    index = lax.broadcasted_iota(jnp.int32, (rows_e, LANES), 0).astype(jnp.float32) + base
    hits = jnp.zeros((rows_e, LANES), jnp.float32)
    for t in range(n_tp):
        for d in range(n_dp):
            ids = share[t, trace_at + 3 + d : trace_at + 4 + d, :]
            hits = hits + jnp.where(index == ids, 1.0, 0.0)
    scale = 1.0 / (jnp.sum(hits, axis=1, keepdims=True) + damp_root * ratio_e)

    e_load.wait()
    stores = []
    for p in range(e_parts):
        for i in range(p * n_g // e_parts, (p + 1) * n_g // e_parts):
            at = slice(i * LANES, (i + 1) * LANES)
            factor = blocks_right(*inverses[n_a + n_g + i])
            e_done[:, at] = split_times(split(e_in[:, at]), factor) * scale
        cols = pl.ds(p * e_cols, e_cols)
        stores.append(
            pltpu.make_async_copy(e_done.at[:, cols], e_out.at[:, cols], e_out_sem.at[p])
        )
        stores[-1].start()
    per_chunk = chunk // LANES
    for c in range(chunks):
        w_loads[c].wait()
        for i in range(c * per_chunk, (c + 1) * per_chunk):
            rows = slice(i * LANES, (i + 1) * LANES)
            factor = blocks_left(*inverses[n_a + i])
            both = jnp.dot(
                factor,
                jnp.concatenate(split(w_in[rows, :]), axis=0),
                preferred_element_type=jnp.float32,
            )
            left = both[:LANES] + both[LANES:]
            for h in range(n_a):
                at = slice(h * LANES, (h + 1) * LANES)
                w_done[rows, at] = split_times(split(left[:, at]), right_a[h])
        rows = pl.ds(c * chunk, chunk)
        stores.append(
            pltpu.make_async_copy(w_done.at[rows], w_out.at[rows], w_out_sem.at[c])
        )
        stores[-1].start()
    for store in stores:
        store.wait()


def invert_apply(own, shared, tile, grad_e, sizes):
    n_tp = shared.shape[0]
    chunk = sizes[-1]
    tile_rows, inner_part = tile.shape
    rows_e, width = grad_e.shape
    vmem = pl.BlockSpec(memory_space=pltpu.VMEM)
    hbm = pl.BlockSpec(memory_space=pltpu.HBM)
    return pl.pallas_call(
        functools.partial(invert_apply_kernel, sizes),
        in_specs=[vmem, hbm, hbm, hbm],
        out_specs=[hbm, hbm],
        out_shape=[
            jax.ShapeDtypeStruct((tile_rows, inner_part), jnp.float32),
            jax.ShapeDtypeStruct((rows_e, width), jnp.float32),
        ],
        scratch_shapes=[
            pltpu.VMEM(shared.shape, jnp.float32),
            pltpu.VMEM(tile.shape, jnp.float32),
            pltpu.VMEM(grad_e.shape, jnp.float32),
            pltpu.VMEM(tile.shape, jnp.float32),
            pltpu.VMEM(grad_e.shape, jnp.float32),
            pltpu.SemaphoreType.DMA,
            pltpu.SemaphoreType.DMA((tile_rows // chunk,)),
            pltpu.SemaphoreType.DMA,
            pltpu.SemaphoreType.DMA((tile_rows // chunk,)),
            pltpu.SemaphoreType.DMA((2,)),
        ],
        compiler_params=pltpu.CompilerParams(vmem_limit_bytes=32 * 1024 * 1024),
        cost_estimate=small_cost(),
        name="invert_apply",
    )(own, shared, tile, grad_e)


def local(acts, out_cot, emb_ids, emb_cot, grad_w, grad_e):
    n_dp = lax.axis_size("dp")
    n_tp = lax.axis_size("tensor")
    layers, tok_rows, inner_part = acts.shape
    width_part = out_cot.shape[2]
    width = width_part * n_tp
    rows_e = grad_e.shape[0]
    tile_rows = grad_w.shape[0] * n_tp
    direct = (
        layers == n_dp
        and n_dp > 1
        and n_dp & (n_dp - 1) == 0
        and tile_rows == width
        and inner_part % (4 * LANES) == 0
        and width_part % (2 * LANES) == 0
        and n_tp % 2 == 0
        and emb_ids.shape[0] < LANES
        and rows_e % ROWS == 0
    )
    if not direct:
        return general_local(acts, out_cot, emb_ids, emb_cot, grad_w, grad_e)
    quads_a = inner_part // (2 * LANES)
    quads_g = width_part // (2 * LANES)
    half = n_dp // 2

    def trade(value, k):
        return lax.ppermute(value, "dp", [(i, i ^ k) for i in range(n_dp)])

    *parts, sending = grams(
        acts, out_cot, emb_cot, emb_ids, grad_w, lax.axis_index("dp"), n_dp, n_tp, quads_a, quads_g
    )
    tile = lax.all_to_all(sending, "tensor", split_axis=0, concat_axis=0, tiled=True)
    tile = tile.reshape(tile_rows, inner_part)
    arrived = [parts[0]] + [trade(parts[k], k) for k in range(1, half)]
    kept_rows = round_up((quads_a + 2 * quads_g) * (HEAD + 1) + half, ROWS)
    kept, mirror = pl.pallas_call(
        functools.partial(half_sum_kernel, quads_a + quads_g, quads_g),
        out_shape=[jax.ShapeDtypeStruct((kept_rows, LANES), jnp.float32)] * 2,
        cost_estimate=small_cost(),
        name="half_sums",
    )(*arrived)
    came = trade(mirror, half)
    own_rows = round_up(quads_a * (HEAD + 1), ROWS)
    share_rows = round_up(2 * quads_g * (HEAD + 1) + 3 + n_dp, ROWS)
    own, share = pl.pallas_call(
        functools.partial(sum_kernel, quads_a, quads_g, half),
        out_shape=[
            jax.ShapeDtypeStruct((own_rows, LANES), jnp.float32),
            jax.ShapeDtypeStruct((share_rows, LANES), jnp.float32),
        ],
        cost_estimate=small_cost(),
        name="sums",
    )(kept, came)
    shared = lax.all_gather(share[None], "tensor", axis=0, tiled=True)
    sizes = (
        quads_a,
        quads_g,
        n_tp,
        n_dp,
        tok_rows * n_dp,
        rows_e * n_dp * n_tp,
        inner_part * n_tp,
        width,
        2 * LANES,
    )
    return tuple(invert_apply(own, shared, tile, grad_e, sizes))


def solution(mesh):
    in_specs = (
        P(None, "dp", "tensor"),
        P(None, "dp", "tensor"),
        P(("dp", "tensor")),
        P("dp", "tensor"),
        P(("dp", "tensor"), None),
        P(("dp", "tensor"), None),
    )
    out_specs = (P("dp", "tensor"), P(("dp", "tensor"), None))
    return jax.shard_map(local, mesh=mesh, in_specs=in_specs, out_specs=out_specs, check_vma=False)
```

```python
import functools

import jax
import jax.numpy as jnp
from jax import lax
from jax.experimental import pallas as pl
from jax.experimental.pallas import tpu as pltpu
from jax.sharding import PartitionSpec as P

HEAD = 64
NS_ITERS = 4
LANES = 128
HALF = HEAD
ROWS = 8


damp_root = 0.7


def newton_inverse(matrices):
    size = matrices.shape[-1]
    eye = jnp.eye(size, dtype=jnp.float32)
    bound = jnp.max(jnp.sum(jnp.abs(matrices), axis=-1), axis=-1)
    approx = eye[None] / bound[:, None, None]
    for sweep in range(NS_ITERS):
        image = jnp.einsum("bij,bjk->bik", matrices, approx, precision=lax.Precision.HIGHEST)
        approx = jnp.einsum(
            "bij,bjk->bik", approx, 2.0 * eye[None] - image, precision=lax.Precision.HIGHEST
        )
    return approx


def general_local(acts, out_cot, emb_ids, emb_cot, grad_w, grad_e):
    n_dp = lax.axis_size("dp")
    n_tp = lax.axis_size("tensor")
    layers, tok_rows, inner_part = acts.shape
    width_part = out_cot.shape[2]
    heads_part = inner_part // HEAD
    groups_part = width_part // HEAD
    tokens_all = tok_rows * n_dp
    width = width_part * n_tp
    inner = inner_part * n_tp
    groups_all = width // HEAD
    rows_e = grad_e.shape[0]
    vocab = rows_e * n_dp * n_tp
    dp_index = lax.axis_index("dp")
    flat_index = dp_index * n_tp + lax.axis_index("tensor")
    tile_rows = grad_w.shape[0] * n_tp
    block_rows = tile_rows // HEAD
    layer_rows = min(tile_rows, width)
    layer_span = tile_rows // layer_rows
    first_layer = dp_index * tile_rows // width
    split_acts = acts.reshape(layers, tok_rows, heads_part, HEAD)
    gram_a = jnp.einsum(
        "lthi,lthj->lhij", split_acts, split_acts, preferred_element_type=jnp.float32
    )
    split_cot = out_cot.reshape(layers, tok_rows, groups_part, HEAD)
    gram_g = jnp.einsum("lthi,lthj->lhij", split_cot, split_cot, preferred_element_type=jnp.float32)
    split_emb = emb_cot.reshape(tok_rows, groups_part, HEAD)
    gram_e = jnp.einsum("thi,thj->hij", split_emb, split_emb, preferred_element_type=jnp.float32)
    blocks = jnp.concatenate(
        [gram_a.reshape(-1, HEAD, HEAD), gram_g.reshape(-1, HEAD, HEAD), gram_e], axis=0
    )
    block_count = blocks.shape[0]
    diagonal_sums = jnp.trace(blocks, axis1=1, axis2=2)
    local_a = jnp.sum(diagonal_sums[: layers * heads_part].reshape(layers, heads_part), axis=1)
    local_g = jnp.sum(
        diagonal_sums[layers * heads_part : layers * (heads_part + groups_part)].reshape(
            layers, groups_part
        ),
        axis=1,
    )
    local_e = jnp.sum(diagonal_sums[layers * (heads_part + groups_part) :])
    trace_local = jnp.concatenate([local_a, local_g, local_e[None]])
    local_counts = jnp.sum(
        (emb_ids[:, None] == jnp.arange(vocab, dtype=jnp.int32)[None, :]).astype(jnp.float32),
        axis=0,
    )
    traces, counts_all = lax.psum((trace_local, local_counts), ("dp", "tensor"))
    counts_mine = lax.dynamic_slice_in_dim(counts_all, flat_index * rows_e, rows_e)
    trace_a = traces[:layers]
    trace_g = traces[layers : 2 * layers]
    trace_e = traces[2 * layers]
    ratio = jnp.sqrt(trace_a / (tokens_all * inner) / (trace_g / (tokens_all * width)))
    ratio_e = jnp.sqrt(tokens_all / vocab / (trace_e / (tokens_all * width)))
    shift = jnp.concatenate(
        [
            jnp.repeat(damp_root * ratio, heads_part),
            jnp.repeat(damp_root / ratio, groups_part),
            jnp.full((groups_part,), 1.0, jnp.float32) * (damp_root / ratio_e),
        ]
    )
    eye = jnp.eye(HEAD, dtype=jnp.float32)
    owned = -(-block_count // n_dp)
    slots = owned * n_dp
    padded = jnp.pad(blocks.reshape(block_count, HEAD * HEAD), ((0, slots - block_count), (0, 0)))
    mine = lax.psum_scatter(padded, "dp", scatter_dimension=0, tiled=True)
    shift_pad = jnp.pad(shift, (0, slots - block_count), constant_values=1.0)
    shift_mine = lax.dynamic_slice_in_dim(shift_pad, dp_index * owned, owned)
    damped = mine.reshape(owned, HEAD, HEAD) / tokens_all + shift_mine[:, None, None] * eye
    inverse_mine = newton_inverse(damped)
    gathered = lax.all_gather(inverse_mine.reshape(owned, HEAD * HEAD), "dp", axis=0, tiled=True)
    inverses = gathered[:block_count].reshape(block_count, HEAD, HEAD)
    inv_a = inverses[: layers * heads_part].reshape(layers, heads_part, HEAD, HEAD)
    inv_g_part = inverses[layers * heads_part : layers * (heads_part + groups_part)].reshape(
        layers, groups_part, HEAD * HEAD
    )
    inv_e_part = inverses[layers * (heads_part + groups_part) :].reshape(groups_part, HEAD * HEAD)
    base_layer = 0
    sending = jnp.concatenate(
        [inv_g_part.reshape(layers * groups_part, HEAD * HEAD), inv_e_part], axis=0
    )
    shared = lax.all_gather(sending[None], "tensor", axis=0, tiled=True)
    inv_g = shared[:, : layers * groups_part].reshape(n_tp, layers, groups_part, HEAD, HEAD)
    inv_g = jnp.transpose(inv_g, (1, 0, 2, 3, 4)).reshape(layers * groups_all, HEAD, HEAD)
    inv_e = shared[:, layers * groups_part :].reshape(groups_all, HEAD, HEAD)
    tile = lax.all_to_all(grad_w, "tensor", split_axis=1, concat_axis=0, tiled=True)
    g_sel = lax.dynamic_slice_in_dim(
        inv_g, dp_index * block_rows - base_layer * groups_all, block_rows, 0
    )
    left = jnp.einsum(
        "bij,bjc->bic",
        g_sel,
        tile.reshape(block_rows, HEAD, inner_part),
        precision=lax.Precision.HIGHEST,
    )
    a_sel = lax.dynamic_slice_in_dim(inv_a, first_layer, layer_span, 0)
    right = jnp.einsum(
        "lrhi,lhij->lrhj",
        left.reshape(layer_span, layer_rows, heads_part, HEAD),
        a_sel,
        precision=lax.Precision.HIGHEST,
    )
    update_w = right.reshape(tile_rows, inner_part)
    scaled = jnp.einsum(
        "rgi,gij->rgj",
        grad_e.reshape(rows_e, groups_all, HEAD),
        inv_e,
        precision=lax.Precision.HIGHEST,
    )
    update_e = scaled.reshape(rows_e, width) / (counts_mine + damp_root * ratio_e)[:, None]
    return (update_w, update_e)


def pair_masks():
    row = lax.broadcasted_iota(jnp.int32, (HEAD, LANES), 0)
    lane = lax.broadcasted_iota(jnp.int32, (HEAD, LANES), 1)
    col = jnp.where(lane < HALF, lane, lane - HALF)
    return row, lane, col


def gram_pair(rows):
    full = lax.dot_general(
        rows, rows, (((0,), (0,)), ((), ())), preferred_element_type=jnp.float32
    )
    _, lane, _ = pair_masks()
    return jnp.where(lane < HALF, full[:HEAD], full[HEAD:])


def pack_quad(first, second):
    row, _, col = pair_masks()
    quad = jnp.where(col >= row, first, second)
    diagonal = jnp.sum(jnp.where(col == row, second, 0.0), axis=0, keepdims=True)
    return quad, diagonal


def unpack_quads(quad_a, diag_a, quad_b, diag_b):
    row, lane, col = pair_masks()
    turned = jnp.concatenate([quad_a, quad_b], axis=0).T
    top, low = turned[:HEAD], turned[HEAD:]
    turn_a = jnp.where(lane < HALF, top, pltpu.roll(low, HALF, 1))
    turn_b = jnp.where(lane < HALF, pltpu.roll(top, HALF, 1), low)

    def both(quad, turn, diag):
        first = jnp.where(col >= row, quad, turn)
        second = jnp.where(col < row, quad, jnp.where(col == row, diag, turn))
        return first, second

    return both(quad_a, turn_a, diag_a) + both(quad_b, turn_b, diag_b)


def split(value):
    high = value.astype(jnp.bfloat16)
    low = (value - high.astype(jnp.float32)).astype(jnp.bfloat16)
    return high, low


def block_diagonal(pair):
    row = lax.broadcasted_iota(jnp.int32, (LANES, LANES), 0)
    lane = lax.broadcasted_iota(jnp.int32, (LANES, LANES), 1)
    double = jnp.concatenate([pair, pair], axis=0)
    return jnp.where((row < HALF) == (lane < HALF), double, jnp.zeros_like(double))


def blocks_right(high, low):
    wide = jnp.concatenate([block_diagonal(high), block_diagonal(low)], axis=1)
    return jnp.concatenate([wide, wide], axis=0)


def blocks_left(high, low):
    high, low = block_diagonal(high), block_diagonal(low)
    return jnp.concatenate(
        [jnp.concatenate([high, high], axis=1), jnp.concatenate([low, low], axis=1)], axis=0
    )


def add_halves(both):
    return both[:, :LANES] + both[:, LANES:]


def split_times(parts, factor):
    return add_halves(
        jnp.dot(jnp.concatenate(parts, axis=1), factor, preferred_element_type=jnp.float32)
    )


def gram_kernel(counts, me_ref, ids_ref, acts_hbm, cot_hbm, emb_hbm, w_hbm, *refs):
    quads_a, quads_g, n_dp, n_tp = counts
    half = n_dp // 2
    outs_hbm, w_out = refs[:half], refs[half]
    acts, cot, emb, w, outs, acts_sem, cot_sem, emb_sem, w_sem, move_sem, out_sem = refs[half + 1 :]
    me = me_ref[0]
    order = [k for j in list(range(1, half)) + [0] for k in (j, j + half)]

    def fetch(k):
        layer = lax.bitwise_xor(me, k)
        return (
            pltpu.make_async_copy(acts_hbm.at[layer], acts.at[k], acts_sem.at[k]),
            pltpu.make_async_copy(cot_hbm.at[layer], cot.at[k], cot_sem.at[k]),
        )

    emb_copy = pltpu.make_async_copy(emb_hbm, emb, emb_sem)
    emb_copy.start()
    for k in order[:2]:
        for copy in fetch(k):
            copy.start()
    part = w_hbm.shape[1] // n_tp
    loads = [
        pltpu.make_async_copy(
            w_hbm.at[:, pl.ds(t * part, part)], w.at[t], w_sem.at[t]
        )
        for t in range(n_tp)
    ]
    for load in loads:
        load.start()
    for k in order[2:]:
        for copy in fetch(k):
            copy.start()
    moves = [
        pltpu.make_async_copy(w.at[t], w_out.at[t], move_sem.at[t]) for t in range(n_tp)
    ]

    def pack(source, at):
        first = gram_pair(source[:, at * 2 * LANES : (at * 2 + 1) * LANES])
        second = gram_pair(source[:, (at * 2 + 1) * LANES : (at * 2 + 2) * LANES])
        return pack_quad(first, second)

    emb_copy.wait()
    emb_rows = emb[...]
    packed_e = [pack(emb_rows, q) for q in range(quads_g)]
    ids = jnp.concatenate(
        [
            ids_ref[...].astype(jnp.float32),
            jnp.full((1, LANES - ids_ref.shape[1]), -1.0, jnp.float32),
        ],
        axis=1,
    )
    stores = []
    for j in list(range(1, half)) + [0]:
        packed = []
        for k in (j, j + half):
            for copy in fetch(k):
                copy.wait()
            rows_a, rows_g = acts[k], cot[k]
            packed += [pack(rows_a, q) for q in range(quads_a)]
            packed += [pack(rows_g, q) for q in range(quads_g)]
        packed += packed_e
        for q, (quad, diagonal) in enumerate(packed):
            outs[j, q * HEAD : (q + 1) * HEAD, :] = quad
            at = len(packed) * HEAD + q
            outs[j, at : at + 1, :] = diagonal
        at = len(packed) * (HEAD + 1)
        outs[j, at : at + 1, :] = ids
        stores.append(pltpu.make_async_copy(outs.at[j], outs_hbm[j], out_sem.at[j]))
        stores[-1].start()
        if j == 1 % half:
            for load, move in zip(loads, moves):
                load.wait()
                move.start()
    for copy in moves + stores:
        copy.wait()


def small_cost():
    return pl.CostEstimate(flops=1000, bytes_accessed=1000, transcendentals=0)


def round_up(value, unit):
    return -(-value // unit) * unit


def grams(acts, out_cot, emb_cot, emb_ids, grad_w, dp_index, n_dp, n_tp, quads_a, quads_g):
    layers, rows, width_a = acts.shape
    width_g = out_cot.shape[2]
    half = n_dp // 2
    payload_rows = round_up((2 * (quads_a + quads_g) + quads_g) * (HEAD + 1) + 1, ROWS)
    part = grad_w.shape[1] // n_tp
    vmem = pl.BlockSpec(memory_space=pltpu.VMEM)
    hbm = pl.BlockSpec(memory_space=pltpu.HBM)
    return pl.pallas_call(
        functools.partial(gram_kernel, (quads_a, quads_g, n_dp, n_tp)),
        in_specs=[pl.BlockSpec(memory_space=pltpu.SMEM), vmem, hbm, hbm, hbm, hbm],
        out_specs=[hbm] * (half + 1),
        out_shape=[jax.ShapeDtypeStruct((payload_rows, LANES), jnp.float32)] * half
        + [jax.ShapeDtypeStruct((n_tp, grad_w.shape[0], part), jnp.float32)],
        scratch_shapes=[
            pltpu.VMEM((layers, rows, width_a), jnp.bfloat16),
            pltpu.VMEM((layers, rows, width_g), jnp.bfloat16),
            pltpu.VMEM((rows, width_g), jnp.bfloat16),
            pltpu.VMEM((n_tp, grad_w.shape[0], part), jnp.float32),
            pltpu.VMEM((half, payload_rows, LANES), jnp.float32),
            pltpu.SemaphoreType.DMA((layers,)),
            pltpu.SemaphoreType.DMA((layers,)),
            pltpu.SemaphoreType.DMA,
            pltpu.SemaphoreType.DMA((n_tp,)),
            pltpu.SemaphoreType.DMA((n_tp,)),
            pltpu.SemaphoreType.DMA((half,)),
        ],
        compiler_params=pltpu.CompilerParams(vmem_limit_bytes=62 * 1024 * 1024),
        cost_estimate=small_cost(),
        name="grams",
    )(dp_index.reshape(1), emb_ids.reshape(1, -1), acts, out_cot, emb_cot, grad_w)


def half_sum_kernel(quads_layer, quads_g, *refs):
    parts, outs = refs[:-2], refs[-2:]
    quads_in = 2 * quads_layer + quads_g
    quads_out = quads_layer + quads_g

    def total(at, size):
        value = parts[0][at : at + size, :]
        for part in parts[1:]:
            value = value + part[at : at + size, :]
        return value

    shared = [
        (total(q * HEAD, HEAD), total(quads_in * HEAD + q, 1))
        for q in range(2 * quads_layer, quads_in)
    ]
    for place, out in enumerate(outs):
        both = [
            (total(q * HEAD, HEAD), total(quads_in * HEAD + q, 1))
            for q in range(place * quads_layer, (place + 1) * quads_layer)
        ]
        for q, (quad, diagonal) in enumerate(both + shared):
            out[q * HEAD : (q + 1) * HEAD, :] = quad
            out[quads_out * HEAD + q : quads_out * HEAD + q + 1, :] = diagonal
        at = quads_out * (HEAD + 1)
        for i, part in enumerate(parts):
            ids_at = quads_in * (HEAD + 1)
            out[at + i : at + i + 1, :] = part[ids_at : ids_at + 1, :]


def sum_kernel(quads_a, quads_g, half, kept, came, own_ref, share_ref):
    quads = quads_a + 2 * quads_g
    diag_at = quads * HEAD
    row, _, col = pair_masks()
    traces = []
    first = 0
    for count, where in ((quads_a, own_ref), (quads_g, share_ref), (quads_g, share_ref)):
        trace = jnp.zeros((1, LANES), jnp.float32)
        for q in range(first, first + count):
            at = slice(q * HEAD, (q + 1) * HEAD)
            quad = kept[at, :] + came[at, :]
            at = slice(diag_at + q, diag_at + q + 1)
            diagonal = kept[at, :] + came[at, :]
            trace = trace + diagonal
            trace = trace + jnp.sum(jnp.where(col == row, quad, 0.0), axis=0, keepdims=True)
            if where is own_ref:
                own_ref[q * HEAD : (q + 1) * HEAD, :] = quad
                own_ref[quads_a * HEAD + q : quads_a * HEAD + q + 1, :] = diagonal
            else:
                at = q - quads_a
                share_ref[at * HEAD : (at + 1) * HEAD, :] = quad
                share_ref[2 * quads_g * HEAD + at : 2 * quads_g * HEAD + at + 1, :] = diagonal
        traces.append(trace)
        first += count
    at = 2 * quads_g * (HEAD + 1)
    for trace in traces:
        share_ref[at : at + 1, :] = trace
        at += 1
    for ref in (kept, came):
        for i in range(half):
            ids_at = quads * (HEAD + 1) + i
            share_ref[at : at + 1, :] = ref[ids_at : ids_at + 1, :]
            at += 1


def invert_apply_kernel(sizes, own_ref, share_hbm, w_hbm, e_hbm, w_out, e_out, *scratch):
    quads_a, quads_g, n_tp, n_dp, tokens, vocab, inner, width, chunk = sizes
    share, w_in, e_in, w_done, e_done, share_sem, w_sem, e_sem, w_out_sem, e_out_sem = scratch
    tile_rows, inner_part = w_in.shape
    rows_e = e_in.shape[0]
    chunks = tile_rows // chunk
    e_parts = 2
    e_cols = width // e_parts
    share_copy = pltpu.make_async_copy(share_hbm, share, share_sem)
    w_loads = [
        pltpu.make_async_copy(
            w_hbm.at[pl.ds(c * chunk, chunk)], w_in.at[pl.ds(c * chunk, chunk)], w_sem.at[c]
        )
        for c in range(chunks)
    ]
    e_load = pltpu.make_async_copy(e_hbm, e_in, e_sem)
    share_copy.start()
    e_load.start()
    for load in w_loads:
        load.start()
    share_copy.wait()

    trace_at = 2 * quads_g * (HEAD + 1)

    def trace_of(kind):
        value = share[0, trace_at + kind : trace_at + kind + 1, :]
        for t in range(1, n_tp):
            value = value + share[t, trace_at + kind : trace_at + kind + 1, :]
        return jnp.sum(value, axis=1, keepdims=True)

    trace_a, trace_g, trace_e = trace_of(0), trace_of(1), trace_of(2)
    ratio = jnp.sqrt(trace_a / (tokens * inner) / (trace_g / (tokens * width)))
    ratio_e = jnp.sqrt(tokens / vocab / (trace_e / (tokens * width)))

    loaded = [
        (
            own_ref[q * HEAD : (q + 1) * HEAD, :],
            own_ref[quads_a * HEAD + q : quads_a * HEAD + q + 1, :],
        )
        for q in range(quads_a)
    ]
    diag_at = 2 * quads_g * HEAD
    for kind in range(2):
        for t in range(n_tp):
            for q in range(kind * quads_g, (kind + 1) * quads_g):
                loaded.append(
                    (
                        share[t, q * HEAD : (q + 1) * HEAD, :],
                        share[t, diag_at + q : diag_at + q + 1, :],
                    )
                )
    pairs = []
    for i in range(0, len(loaded), 2):
        pairs += unpack_quads(*loaded[i], *loaded[i + 1])
    n_a, n_g = 2 * quads_a, 2 * quads_g * n_tp

    row, lane, col = pair_masks()
    eye = jnp.where(col == row, 1.0, 0.0)
    low_lane = lane[:1] < HALF
    shifts = [damp_root * ratio] * n_a + [damp_root / ratio] * n_g + [damp_root / ratio_e] * n_g
    images, over = [], []
    for pair, shift in zip(pairs, shifts):
        damped = pair * (1.0 / tokens) + shift * eye
        sums = jnp.sum(jnp.abs(damped), axis=0, keepdims=True)
        bound = jnp.where(
            low_lane,
            jnp.max(jnp.where(low_lane, sums, 0.0), axis=1, keepdims=True),
            jnp.max(jnp.where(low_lane, 0.0, sums), axis=1, keepdims=True),
        )
        inverse_bound = 1.0 / bound
        images.append(damped * inverse_bound)
        over.append(inverse_bound)
    approx = [2.0 * eye - image for image in images]
    for sweep in range(NS_ITERS):
        splits = [split(image) for image in images]
        factors = [blocks_right(*parts) for parts in splits]
        if sweep == 0:
            images = [
                2.0 * image - split_times(parts, factor)
                for image, parts, factor in zip(images, splits, factors)
            ]
        elif sweep < NS_ITERS - 1:
            products = []
            for value, parts, factor in zip(approx, splits, factors):
                stacked = [
                    jnp.concatenate([a, b], axis=0) for a, b in zip(split(value), parts)
                ]
                products.append(split_times(stacked, factor))
            approx = [2.0 * a - p[:HEAD] for a, p in zip(approx, products)]
            images = [2.0 * b - p[HEAD:] for b, p in zip(images, products)]
        else:
            approx = [
                2.0 * a - split_times(split(a), factor) for a, factor in zip(approx, factors)
            ]
    inverses = [split(a * b) for a, b in zip(approx, over)]
    right_a = [blocks_right(*parts) for parts in inverses[:n_a]]

    base = ((lax.axis_index("dp") * n_tp + lax.axis_index("tensor")) * rows_e).astype(jnp.float32)
    index = lax.broadcasted_iota(jnp.int32, (rows_e, LANES), 0).astype(jnp.float32) + base
    hits = jnp.zeros((rows_e, LANES), jnp.float32)
    for t in range(n_tp):
        for d in range(n_dp):
            ids = share[t, trace_at + 3 + d : trace_at + 4 + d, :]
            hits = hits + jnp.where(index == ids, 1.0, 0.0)
    scale = 1.0 / (jnp.sum(hits, axis=1, keepdims=True) + damp_root * ratio_e)

    e_load.wait()
    stores = []
    for p in range(e_parts):
        for i in range(p * n_g // e_parts, (p + 1) * n_g // e_parts):
            at = slice(i * LANES, (i + 1) * LANES)
            factor = blocks_right(*inverses[n_a + n_g + i])
            e_done[:, at] = split_times(split(e_in[:, at]), factor) * scale
        cols = pl.ds(p * e_cols, e_cols)
        stores.append(
            pltpu.make_async_copy(e_done.at[:, cols], e_out.at[:, cols], e_out_sem.at[p])
        )
        stores[-1].start()
    per_chunk = chunk // LANES
    for c in range(chunks):
        w_loads[c].wait()
        for i in range(c * per_chunk, (c + 1) * per_chunk):
            rows = slice(i * LANES, (i + 1) * LANES)
            factor = blocks_left(*inverses[n_a + i])
            both = jnp.dot(
                factor,
                jnp.concatenate(split(w_in[rows, :]), axis=0),
                preferred_element_type=jnp.float32,
            )
            left = both[:LANES] + both[LANES:]
            for h in range(n_a):
                at = slice(h * LANES, (h + 1) * LANES)
                w_done[rows, at] = split_times(split(left[:, at]), right_a[h])
        rows = pl.ds(c * chunk, chunk)
        stores.append(
            pltpu.make_async_copy(w_done.at[rows], w_out.at[rows], w_out_sem.at[c])
        )
        stores[-1].start()
    for store in stores:
        store.wait()


def invert_apply(own, shared, tile, grad_e, sizes):
    n_tp = shared.shape[0]
    chunk = sizes[-1]
    tile_rows, inner_part = tile.shape
    rows_e, width = grad_e.shape
    vmem = pl.BlockSpec(memory_space=pltpu.VMEM)
    hbm = pl.BlockSpec(memory_space=pltpu.HBM)
    return pl.pallas_call(
        functools.partial(invert_apply_kernel, sizes),
        in_specs=[vmem, hbm, hbm, hbm],
        out_specs=[hbm, hbm],
        out_shape=[
            jax.ShapeDtypeStruct((tile_rows, inner_part), jnp.float32),
            jax.ShapeDtypeStruct((rows_e, width), jnp.float32),
        ],
        scratch_shapes=[
            pltpu.VMEM(shared.shape, jnp.float32),
            pltpu.VMEM(tile.shape, jnp.float32),
            pltpu.VMEM(grad_e.shape, jnp.float32),
            pltpu.VMEM(tile.shape, jnp.float32),
            pltpu.VMEM(grad_e.shape, jnp.float32),
            pltpu.SemaphoreType.DMA,
            pltpu.SemaphoreType.DMA((tile_rows // chunk,)),
            pltpu.SemaphoreType.DMA,
            pltpu.SemaphoreType.DMA((tile_rows // chunk,)),
            pltpu.SemaphoreType.DMA((2,)),
        ],
        compiler_params=pltpu.CompilerParams(vmem_limit_bytes=32 * 1024 * 1024),
        cost_estimate=small_cost(),
        name="invert_apply",
    )(own, shared, tile, grad_e)


def local(acts, out_cot, emb_ids, emb_cot, grad_w, grad_e):
    n_dp = lax.axis_size("dp")
    n_tp = lax.axis_size("tensor")
    layers, tok_rows, inner_part = acts.shape
    width_part = out_cot.shape[2]
    width = width_part * n_tp
    rows_e = grad_e.shape[0]
    tile_rows = grad_w.shape[0] * n_tp
    direct = (
        layers == n_dp
        and n_dp > 1
        and n_dp & (n_dp - 1) == 0
        and tile_rows == width
        and inner_part % (4 * LANES) == 0
        and width_part % (2 * LANES) == 0
        and n_tp % 2 == 0
        and emb_ids.shape[0] < LANES
        and rows_e % ROWS == 0
    )
    if not direct:
        return general_local(acts, out_cot, emb_ids, emb_cot, grad_w, grad_e)
    quads_a = inner_part // (2 * LANES)
    quads_g = width_part // (2 * LANES)
    half = n_dp // 2
    vmem = pl.BlockSpec(memory_space=pltpu.VMEM)

    def trade(value, k):
        return lax.ppermute(value, "dp", [(i, i ^ k) for i in range(n_dp)])

    *parts, sending = grams(
        acts, out_cot, emb_cot, emb_ids, grad_w, lax.axis_index("dp"), n_dp, n_tp, quads_a, quads_g
    )
    tile = lax.all_to_all(sending, "tensor", split_axis=0, concat_axis=0, tiled=True)
    tile = tile.reshape(tile_rows, inner_part)
    arrived = [parts[0]] + [trade(parts[k], k) for k in range(1, half)]
    kept_rows = round_up((quads_a + 2 * quads_g) * (HEAD + 1) + half, ROWS)
    kept, mirror = pl.pallas_call(
        functools.partial(half_sum_kernel, quads_a + quads_g, quads_g),
        in_specs=[vmem] * half,
        out_specs=[vmem] * 2,
        out_shape=[jax.ShapeDtypeStruct((kept_rows, LANES), jnp.float32)] * 2,
        compiler_params=pltpu.CompilerParams(vmem_limit_bytes=8 * 1024 * 1024),
        cost_estimate=small_cost(),
        name="half_sums",
    )(*arrived)
    came = trade(mirror, half)
    own_rows = round_up(quads_a * (HEAD + 1), ROWS)
    share_rows = round_up(2 * quads_g * (HEAD + 1) + 3 + n_dp, ROWS)
    own, share = pl.pallas_call(
        functools.partial(sum_kernel, quads_a, quads_g, half),
        in_specs=[vmem] * 2,
        out_specs=[vmem] * 2,
        out_shape=[
            jax.ShapeDtypeStruct((own_rows, LANES), jnp.float32),
            jax.ShapeDtypeStruct((share_rows, LANES), jnp.float32),
        ],
        compiler_params=pltpu.CompilerParams(vmem_limit_bytes=8 * 1024 * 1024),
        cost_estimate=small_cost(),
        name="sums",
    )(kept, came)
    shared = lax.all_gather(share[None], "tensor", axis=0, tiled=True)
    sizes = (
        quads_a,
        quads_g,
        n_tp,
        n_dp,
        tok_rows * n_dp,
        rows_e * n_dp * n_tp,
        inner_part * n_tp,
        width,
        2 * LANES,
    )
    return tuple(invert_apply(own, shared, tile, grad_e, sizes))


def solution(mesh):
    in_specs = (
        P(None, "dp", "tensor"),
        P(None, "dp", "tensor"),
        P(("dp", "tensor")),
        P("dp", "tensor"),
        P(("dp", "tensor"), None),
        P(("dp", "tensor"), None),
    )
    out_specs = (P("dp", "tensor"), P(("dp", "tensor"), None))
    return jax.shard_map(local, mesh=mesh, in_specs=in_specs, out_specs=out_specs, check_vma=False)
```

```python
import functools

import jax
import jax.numpy as jnp
from jax import lax
from jax.experimental import pallas as pl
from jax.experimental.pallas import tpu as pltpu
from jax.sharding import PartitionSpec as P

HEAD = 64
NS_ITERS = 4
LANES = 128
HALF = HEAD
ROWS = 8


damp_root = 0.7


def newton_inverse(matrices):
    size = matrices.shape[-1]
    eye = jnp.eye(size, dtype=jnp.float32)
    bound = jnp.max(jnp.sum(jnp.abs(matrices), axis=-1), axis=-1)
    approx = eye[None] / bound[:, None, None]
    for sweep in range(NS_ITERS):
        image = jnp.einsum("bij,bjk->bik", matrices, approx, precision=lax.Precision.HIGHEST)
        approx = jnp.einsum(
            "bij,bjk->bik", approx, 2.0 * eye[None] - image, precision=lax.Precision.HIGHEST
        )
    return approx


def general_local(acts, out_cot, emb_ids, emb_cot, grad_w, grad_e):
    n_dp = lax.axis_size("dp")
    n_tp = lax.axis_size("tensor")
    layers, tok_rows, inner_part = acts.shape
    width_part = out_cot.shape[2]
    heads_part = inner_part // HEAD
    groups_part = width_part // HEAD
    tokens_all = tok_rows * n_dp
    width = width_part * n_tp
    inner = inner_part * n_tp
    groups_all = width // HEAD
    rows_e = grad_e.shape[0]
    vocab = rows_e * n_dp * n_tp
    dp_index = lax.axis_index("dp")
    flat_index = dp_index * n_tp + lax.axis_index("tensor")
    tile_rows = grad_w.shape[0] * n_tp
    block_rows = tile_rows // HEAD
    layer_rows = min(tile_rows, width)
    layer_span = tile_rows // layer_rows
    first_layer = dp_index * tile_rows // width
    split_acts = acts.reshape(layers, tok_rows, heads_part, HEAD)
    gram_a = jnp.einsum(
        "lthi,lthj->lhij", split_acts, split_acts, preferred_element_type=jnp.float32
    )
    split_cot = out_cot.reshape(layers, tok_rows, groups_part, HEAD)
    gram_g = jnp.einsum("lthi,lthj->lhij", split_cot, split_cot, preferred_element_type=jnp.float32)
    split_emb = emb_cot.reshape(tok_rows, groups_part, HEAD)
    gram_e = jnp.einsum("thi,thj->hij", split_emb, split_emb, preferred_element_type=jnp.float32)
    blocks = jnp.concatenate(
        [gram_a.reshape(-1, HEAD, HEAD), gram_g.reshape(-1, HEAD, HEAD), gram_e], axis=0
    )
    block_count = blocks.shape[0]
    diagonal_sums = jnp.trace(blocks, axis1=1, axis2=2)
    local_a = jnp.sum(diagonal_sums[: layers * heads_part].reshape(layers, heads_part), axis=1)
    local_g = jnp.sum(
        diagonal_sums[layers * heads_part : layers * (heads_part + groups_part)].reshape(
            layers, groups_part
        ),
        axis=1,
    )
    local_e = jnp.sum(diagonal_sums[layers * (heads_part + groups_part) :])
    trace_local = jnp.concatenate([local_a, local_g, local_e[None]])
    local_counts = jnp.sum(
        (emb_ids[:, None] == jnp.arange(vocab, dtype=jnp.int32)[None, :]).astype(jnp.float32),
        axis=0,
    )
    traces, counts_all = lax.psum((trace_local, local_counts), ("dp", "tensor"))
    counts_mine = lax.dynamic_slice_in_dim(counts_all, flat_index * rows_e, rows_e)
    trace_a = traces[:layers]
    trace_g = traces[layers : 2 * layers]
    trace_e = traces[2 * layers]
    ratio = jnp.sqrt(trace_a / (tokens_all * inner) / (trace_g / (tokens_all * width)))
    ratio_e = jnp.sqrt(tokens_all / vocab / (trace_e / (tokens_all * width)))
    shift = jnp.concatenate(
        [
            jnp.repeat(damp_root * ratio, heads_part),
            jnp.repeat(damp_root / ratio, groups_part),
            jnp.full((groups_part,), 1.0, jnp.float32) * (damp_root / ratio_e),
        ]
    )
    eye = jnp.eye(HEAD, dtype=jnp.float32)
    owned = -(-block_count // n_dp)
    slots = owned * n_dp
    padded = jnp.pad(blocks.reshape(block_count, HEAD * HEAD), ((0, slots - block_count), (0, 0)))
    mine = lax.psum_scatter(padded, "dp", scatter_dimension=0, tiled=True)
    shift_pad = jnp.pad(shift, (0, slots - block_count), constant_values=1.0)
    shift_mine = lax.dynamic_slice_in_dim(shift_pad, dp_index * owned, owned)
    damped = mine.reshape(owned, HEAD, HEAD) / tokens_all + shift_mine[:, None, None] * eye
    inverse_mine = newton_inverse(damped)
    gathered = lax.all_gather(inverse_mine.reshape(owned, HEAD * HEAD), "dp", axis=0, tiled=True)
    inverses = gathered[:block_count].reshape(block_count, HEAD, HEAD)
    inv_a = inverses[: layers * heads_part].reshape(layers, heads_part, HEAD, HEAD)
    inv_g_part = inverses[layers * heads_part : layers * (heads_part + groups_part)].reshape(
        layers, groups_part, HEAD * HEAD
    )
    inv_e_part = inverses[layers * (heads_part + groups_part) :].reshape(groups_part, HEAD * HEAD)
    base_layer = 0
    sending = jnp.concatenate(
        [inv_g_part.reshape(layers * groups_part, HEAD * HEAD), inv_e_part], axis=0
    )
    shared = lax.all_gather(sending[None], "tensor", axis=0, tiled=True)
    inv_g = shared[:, : layers * groups_part].reshape(n_tp, layers, groups_part, HEAD, HEAD)
    inv_g = jnp.transpose(inv_g, (1, 0, 2, 3, 4)).reshape(layers * groups_all, HEAD, HEAD)
    inv_e = shared[:, layers * groups_part :].reshape(groups_all, HEAD, HEAD)
    tile = lax.all_to_all(grad_w, "tensor", split_axis=1, concat_axis=0, tiled=True)
    g_sel = lax.dynamic_slice_in_dim(
        inv_g, dp_index * block_rows - base_layer * groups_all, block_rows, 0
    )
    left = jnp.einsum(
        "bij,bjc->bic",
        g_sel,
        tile.reshape(block_rows, HEAD, inner_part),
        precision=lax.Precision.HIGHEST,
    )
    a_sel = lax.dynamic_slice_in_dim(inv_a, first_layer, layer_span, 0)
    right = jnp.einsum(
        "lrhi,lhij->lrhj",
        left.reshape(layer_span, layer_rows, heads_part, HEAD),
        a_sel,
        precision=lax.Precision.HIGHEST,
    )
    update_w = right.reshape(tile_rows, inner_part)
    scaled = jnp.einsum(
        "rgi,gij->rgj",
        grad_e.reshape(rows_e, groups_all, HEAD),
        inv_e,
        precision=lax.Precision.HIGHEST,
    )
    update_e = scaled.reshape(rows_e, width) / (counts_mine + damp_root * ratio_e)[:, None]
    return (update_w, update_e)


def pair_masks():
    row = lax.broadcasted_iota(jnp.int32, (HEAD, LANES), 0)
    lane = lax.broadcasted_iota(jnp.int32, (HEAD, LANES), 1)
    col = jnp.where(lane < HALF, lane, lane - HALF)
    return row, lane, col


def gram_pair(rows):
    full = lax.dot_general(
        rows, rows, (((0,), (0,)), ((), ())), preferred_element_type=jnp.float32
    )
    _, lane, _ = pair_masks()
    return jnp.where(lane < HALF, full[:HEAD], full[HEAD:])


def pack_quad(first, second):
    row, _, col = pair_masks()
    quad = jnp.where(col >= row, first, second)
    diagonal = jnp.sum(jnp.where(col == row, second, 0.0), axis=0, keepdims=True)
    return quad, diagonal


def unpack_quads(quad_a, diag_a, quad_b, diag_b):
    row, lane, col = pair_masks()
    turned = jnp.concatenate([quad_a, quad_b], axis=0).T
    top, low = turned[:HEAD], turned[HEAD:]
    turn_a = jnp.where(lane < HALF, top, pltpu.roll(low, HALF, 1))
    turn_b = jnp.where(lane < HALF, pltpu.roll(top, HALF, 1), low)

    def both(quad, turn, diag):
        first = jnp.where(col >= row, quad, turn)
        second = jnp.where(col < row, quad, jnp.where(col == row, diag, turn))
        return first, second

    return both(quad_a, turn_a, diag_a) + both(quad_b, turn_b, diag_b)


def split(value):
    high = value.astype(jnp.bfloat16)
    low = (value - high.astype(jnp.float32)).astype(jnp.bfloat16)
    return high, low


def block_diagonal(pair):
    row = lax.broadcasted_iota(jnp.int32, (LANES, LANES), 0)
    lane = lax.broadcasted_iota(jnp.int32, (LANES, LANES), 1)
    double = jnp.concatenate([pair, pair], axis=0)
    return jnp.where((row < HALF) == (lane < HALF), double, jnp.zeros_like(double))


def blocks_right(high, low):
    wide = jnp.concatenate([block_diagonal(high), block_diagonal(low)], axis=1)
    return jnp.concatenate([wide, wide], axis=0)


def blocks_left(high, low):
    high, low = block_diagonal(high), block_diagonal(low)
    return jnp.concatenate(
        [jnp.concatenate([high, high], axis=1), jnp.concatenate([low, low], axis=1)], axis=0
    )


def add_halves(both):
    return both[:, :LANES] + both[:, LANES:]


def split_times(parts, factor):
    return add_halves(
        jnp.dot(jnp.concatenate(parts, axis=1), factor, preferred_element_type=jnp.float32)
    )


def pack_all(source, quads):
    row, _, col = pair_masks()
    packed, trace = [], jnp.zeros((1, LANES), jnp.float32)
    for q in range(quads):
        first = gram_pair(source[:, q * 2 * LANES : (q * 2 + 1) * LANES])
        second = gram_pair(source[:, (q * 2 + 1) * LANES : (q * 2 + 2) * LANES])
        quad, diagonal = pack_quad(first, second)
        packed.append((quad, diagonal))
        trace = trace + diagonal
        trace = trace + jnp.sum(jnp.where(col == row, first, 0.0), axis=0, keepdims=True)
    return packed, trace


def put_packed(out, packed, more=()):
    for q, (quad, diagonal) in enumerate(packed):
        out[q * HEAD : (q + 1) * HEAD, :] = quad
        at = len(packed) * HEAD + q
        out[at : at + 1, :] = diagonal
    for i, line in enumerate(more):
        at = len(packed) * (HEAD + 1) + i
        out[at : at + 1, :] = line


def gram_kernel(counts, ids, acts, cot, emb, after, *outs):
    quads_a, quads_g, n_dp = counts
    half = n_dp // 2
    outs_g, outs_a = outs[:half], outs[half:]
    me = lax.axis_index("dp")
    packed_e, _ = pack_all(emb[...], quads_g)
    ids_row = jnp.concatenate(
        [
            ids[...].astype(jnp.float32),
            jnp.full((1, LANES - ids.shape[1]), -1.0, jnp.float32),
        ],
        axis=1,
    )
    for j in range(half):
        packed_g, packed_a, traces = [], [], []
        for k in (j, j + half):
            layer = lax.bitwise_xor(me, k)
            packed_g += pack_all(cot[layer], quads_g)[0]
            packed, trace = pack_all(acts[layer], quads_a)
            packed_a += packed
            traces.append(trace)
        put_packed(outs_g[j], packed_g + packed_e, traces + [ids_row])
        put_packed(outs_a[j], packed_a)


def small_cost():
    return pl.CostEstimate(flops=1000, bytes_accessed=1000, transcendentals=0)


def round_up(value, unit):
    return -(-value // unit) * unit


def grams(acts, out_cot, emb_cot, emb_ids, after, n_dp, quads_a, quads_g):
    layers, rows, width_a = acts.shape
    width_g = out_cot.shape[2]
    half = n_dp // 2
    rows_g = round_up(3 * quads_g * (HEAD + 1) + 3, ROWS)
    rows_a = round_up(2 * quads_a * (HEAD + 1), ROWS)
    vmem = pl.BlockSpec(memory_space=pltpu.VMEM)
    hbm = pl.BlockSpec(memory_space=pltpu.HBM)
    outs = pl.pallas_call(
        functools.partial(gram_kernel, (quads_a, quads_g, n_dp)),
        in_specs=[vmem] * 4 + [hbm],
        out_specs=[vmem] * (2 * half),
        out_shape=[jax.ShapeDtypeStruct((rows_g, LANES), jnp.float32)] * half
        + [jax.ShapeDtypeStruct((rows_a, LANES), jnp.float32)] * half,
        compiler_params=pltpu.CompilerParams(vmem_limit_bytes=24 * 1024 * 1024),
        cost_estimate=small_cost(),
        name="grams",
    )(emb_ids.reshape(1, -1), acts, out_cot, emb_cot, after)
    return outs[:half], outs[half:]


def column_parts_kernel(n_tp, w_hbm, *refs):
    outs = refs[: n_tp - 1]
    w, load_sem, move_sem = refs[n_tp - 1 :]
    me = lax.axis_index("tensor")
    part = w.shape[2]
    loads, moves = [], []
    for k in range(n_tp - 1, 0, -1):
        at = pl.multiple_of(lax.bitwise_xor(me, k) * part, part)
        loads.append(
            pltpu.make_async_copy(
                w_hbm.at[:, pl.ds(at, part)], w.at[k - 1], load_sem.at[k - 1]
            )
        )
        moves.append(pltpu.make_async_copy(w.at[k - 1], outs[k - 1], move_sem.at[k - 1]))
        loads[-1].start()
    for load, move in zip(loads, moves):
        load.wait()
        move.start()
    for move in moves:
        move.wait()


def column_parts(grad_w, n_tp):
    rows, width = grad_w.shape
    part = (rows, width // n_tp)
    hbm = pl.BlockSpec(memory_space=pltpu.HBM)
    return pl.pallas_call(
        functools.partial(column_parts_kernel, n_tp),
        in_specs=[hbm],
        out_specs=[hbm] * (n_tp - 1),
        out_shape=[jax.ShapeDtypeStruct(part, jnp.float32)] * (n_tp - 1),
        scratch_shapes=[
            pltpu.VMEM((n_tp - 1, *part), jnp.float32),
            pltpu.SemaphoreType.DMA((n_tp - 1,)),
            pltpu.SemaphoreType.DMA((n_tp - 1,)),
        ],
        compiler_params=pltpu.CompilerParams(vmem_limit_bytes=40 * 1024 * 1024),
        cost_estimate=small_cost(),
        name="column_parts",
    )(grad_w)


def total_of(parts, at, size):
    value = parts[0][at : at + size, :]
    for part in parts[1:]:
        value = value + part[at : at + size, :]
    return value


def take_packed(parts, first, count, quads):
    return [
        (total_of(parts, q * HEAD, HEAD), total_of(parts, quads * HEAD + q, 1))
        for q in range(first, first + count)
    ]


def half_sum_a_kernel(quads_a, *refs):
    parts, outs = refs[:-2], refs[-2:]
    for place, out in enumerate(outs):
        put_packed(out, take_packed(parts, place * quads_a, quads_a, 2 * quads_a))


def half_sum_g_kernel(quads_g, *refs):
    parts, outs = refs[:-2], refs[-2:]
    quads = 3 * quads_g
    shared = take_packed(parts, 2 * quads_g, quads_g, quads)
    at = quads * (HEAD + 1)
    ids = [part[at + 2 : at + 3, :] for part in parts]
    for place, out in enumerate(outs):
        own = take_packed(parts, place * quads_g, quads_g, quads)
        put_packed(out, own + shared, [total_of(parts, at + place, 1)] + ids)


def sum_g_kernel(quads_g, half, kept, came, share):
    quads = 2 * quads_g
    row, _, col = pair_masks()
    packed = take_packed((kept, came), 0, quads, quads)
    at = quads * (HEAD + 1)
    traces = [kept[at : at + 1, :] + came[at : at + 1, :]]
    for kind in range(2):
        trace = jnp.zeros((1, LANES), jnp.float32)
        for quad, diagonal in packed[kind * quads_g : (kind + 1) * quads_g]:
            trace = trace + diagonal
            trace = trace + jnp.sum(jnp.where(col == row, quad, 0.0), axis=0, keepdims=True)
        traces.append(trace)
    ids = [ref[at + 1 + i : at + 2 + i, :] for ref in (kept, came) for i in range(half)]
    put_packed(share, packed, traces + ids)


def invert_apply_kernel(sizes, kept_a, came_a, share, e_in, w_hbm, *refs):
    quads_a, quads_g, n_tp, n_dp, tokens, vocab, inner, width = sizes
    came_w, w_out, e_out = refs[: n_tp - 1], refs[n_tp - 1], refs[n_tp]
    w_own, w_done, e_done, w_sem, w_out_sem, e_out_sem = refs[n_tp + 1 :]
    chunk, part = w_own.shape
    rows_e = e_in.shape[0]
    me = lax.axis_index("tensor")
    w_load = pltpu.make_async_copy(
        w_hbm.at[:, pl.ds(pl.multiple_of(me * part, part), part)], w_own, w_sem
    )
    w_load.start()
    w_in = [w_own, *came_w]
    e_parts = 2
    e_cols = width // e_parts
    trace_at = 2 * quads_g * (HEAD + 1)

    def trace_of(kind):
        value = share[0, trace_at + kind : trace_at + kind + 1, :]
        for t in range(1, n_tp):
            value = value + share[t, trace_at + kind : trace_at + kind + 1, :]
        return jnp.sum(value, axis=1, keepdims=True)

    trace_a, trace_g, trace_e = trace_of(0), trace_of(1), trace_of(2)
    ratio = jnp.sqrt(trace_a / (tokens * inner) / (trace_g / (tokens * width)))
    ratio_e = jnp.sqrt(tokens / vocab / (trace_e / (tokens * width)))

    loaded = take_packed((kept_a, came_a), 0, quads_a, quads_a)
    diag_at = 2 * quads_g * HEAD
    for kind in range(2):
        for t in range(n_tp):
            source = lax.bitwise_xor(me, t) if kind == 0 else t
            for q in range(kind * quads_g, (kind + 1) * quads_g):
                loaded.append(
                    (
                        share[source, q * HEAD : (q + 1) * HEAD, :],
                        share[source, diag_at + q : diag_at + q + 1, :],
                    )
                )
    pairs = []
    for i in range(0, len(loaded), 2):
        pairs += unpack_quads(*loaded[i], *loaded[i + 1])
    n_a, n_g = 2 * quads_a, 2 * quads_g * n_tp

    row, lane, col = pair_masks()
    eye = jnp.where(col == row, 1.0, 0.0)
    low_lane = lane[:1] < HALF
    shifts = [damp_root * ratio] * n_a + [damp_root / ratio] * n_g + [damp_root / ratio_e] * n_g
    images, over = [], []
    for pair, shift in zip(pairs, shifts):
        damped = pair * (1.0 / tokens) + shift * eye
        sums = jnp.sum(jnp.abs(damped), axis=0, keepdims=True)
        bound = jnp.where(
            low_lane,
            jnp.max(jnp.where(low_lane, sums, 0.0), axis=1, keepdims=True),
            jnp.max(jnp.where(low_lane, 0.0, sums), axis=1, keepdims=True),
        )
        inverse_bound = 1.0 / bound
        images.append(damped * inverse_bound)
        over.append(inverse_bound)
    approx = [2.0 * eye - image for image in images]
    for sweep in range(NS_ITERS):
        splits = [split(image) for image in images]
        factors = [blocks_right(*parts) for parts in splits]
        if sweep == 0:
            images = [
                2.0 * image - split_times(parts, factor)
                for image, parts, factor in zip(images, splits, factors)
            ]
        elif sweep < NS_ITERS - 1:
            products = []
            for value, parts, factor in zip(approx, splits, factors):
                stacked = [
                    jnp.concatenate([a, b], axis=0) for a, b in zip(split(value), parts)
                ]
                products.append(split_times(stacked, factor))
            approx = [2.0 * a - p[:HEAD] for a, p in zip(approx, products)]
            images = [2.0 * b - p[HEAD:] for b, p in zip(images, products)]
        else:
            approx = [
                2.0 * a - split_times(split(a), factor) for a, factor in zip(approx, factors)
            ]
    inverses = [split(a * b) for a, b in zip(approx, over)]
    right_a = [blocks_right(*parts) for parts in inverses[:n_a]]

    base = ((lax.axis_index("dp") * n_tp + lax.axis_index("tensor")) * rows_e).astype(jnp.float32)
    index = lax.broadcasted_iota(jnp.int32, (rows_e, LANES), 0).astype(jnp.float32) + base
    hits = jnp.zeros((rows_e, LANES), jnp.float32)
    for t in range(n_tp):
        for d in range(n_dp):
            ids = share[t, trace_at + 3 + d : trace_at + 4 + d, :]
            hits = hits + jnp.where(index == ids, 1.0, 0.0)
    scale = 1.0 / (jnp.sum(hits, axis=1, keepdims=True) + damp_root * ratio_e)

    stores = []
    for p in range(e_parts):
        for i in range(p * n_g // e_parts, (p + 1) * n_g // e_parts):
            at = slice(i * LANES, (i + 1) * LANES)
            factor = blocks_right(*inverses[n_a + n_g + i])
            e_done[:, at] = split_times(split(e_in[:, at]), factor) * scale
        cols = pl.ds(p * e_cols, e_cols)
        stores.append(
            pltpu.make_async_copy(e_done.at[:, cols], e_out.at[:, cols], e_out_sem.at[p])
        )
        stores[-1].start()
    per_chunk = chunk // LANES
    for k in range(n_tp):
        if k == 0:
            w_load.wait()
        for i in range(per_chunk):
            rows = slice(i * LANES, (i + 1) * LANES)
            factor = blocks_left(*inverses[n_a + k * per_chunk + i])
            both = jnp.dot(
                factor,
                jnp.concatenate(split(w_in[k][rows, :]), axis=0),
                preferred_element_type=jnp.float32,
            )
            left = both[:LANES] + both[LANES:]
            for h in range(n_a):
                at = slice(h * LANES, (h + 1) * LANES)
                w_done[k, rows, at] = split_times(split(left[:, at]), right_a[h])
        rows = pl.ds(pl.multiple_of(lax.bitwise_xor(me, k) * chunk, chunk), chunk)
        stores.append(pltpu.make_async_copy(w_done.at[k], w_out.at[rows], w_out_sem.at[k]))
        stores[-1].start()
    for store in stores:
        store.wait()


def invert_apply(kept_a, came_a, shared, grad_e, grad_w, came_w, sizes):
    n_tp = len(came_w) + 1
    chunk, part = came_w[0].shape
    rows_e, width = grad_e.shape
    vmem = pl.BlockSpec(memory_space=pltpu.VMEM)
    hbm = pl.BlockSpec(memory_space=pltpu.HBM)
    return pl.pallas_call(
        functools.partial(invert_apply_kernel, sizes),
        in_specs=[vmem] * 4 + [hbm] + [vmem] * (n_tp - 1),
        out_specs=[hbm, hbm],
        out_shape=[
            jax.ShapeDtypeStruct((chunk * n_tp, part), jnp.float32),
            jax.ShapeDtypeStruct((rows_e, width), jnp.float32),
        ],
        scratch_shapes=[
            pltpu.VMEM((chunk, part), jnp.float32),
            pltpu.VMEM((n_tp, chunk, part), jnp.float32),
            pltpu.VMEM(grad_e.shape, jnp.float32),
            pltpu.SemaphoreType.DMA,
            pltpu.SemaphoreType.DMA((n_tp,)),
            pltpu.SemaphoreType.DMA((2,)),
        ],
        compiler_params=pltpu.CompilerParams(vmem_limit_bytes=24 * 1024 * 1024),
        cost_estimate=small_cost(),
        name="invert_apply",
    )(kept_a, came_a, shared, grad_e, grad_w, *came_w)


def add_up(kernel, name, operands, rows):
    vmem = pl.BlockSpec(memory_space=pltpu.VMEM)
    return pl.pallas_call(
        kernel,
        in_specs=[vmem] * len(operands),
        out_specs=[vmem] * len(rows),
        out_shape=[jax.ShapeDtypeStruct((size, LANES), jnp.float32) for size in rows],
        compiler_params=pltpu.CompilerParams(vmem_limit_bytes=8 * 1024 * 1024),
        cost_estimate=small_cost(),
        name=name,
    )(*operands)


def local(acts, out_cot, emb_ids, emb_cot, grad_w, grad_e):
    n_dp = lax.axis_size("dp")
    n_tp = lax.axis_size("tensor")
    layers, tok_rows, inner_part = acts.shape
    width_part = out_cot.shape[2]
    width = width_part * n_tp
    rows_e = grad_e.shape[0]
    tile_rows = grad_w.shape[0] * n_tp
    direct = (
        layers == n_dp
        and n_dp > 1
        and n_dp & (n_dp - 1) == 0
        and tile_rows == width
        and inner_part % (4 * LANES) == 0
        and width_part % (2 * LANES) == 0
        and n_tp > 1
        and n_tp & (n_tp - 1) == 0
        and emb_ids.shape[0] < LANES
        and rows_e % ROWS == 0
    )
    if not direct:
        return general_local(acts, out_cot, emb_ids, emb_cot, grad_w, grad_e)
    quads_a = inner_part // (2 * LANES)
    quads_g = width_part // (2 * LANES)
    half = n_dp // 2

    def trade(value, k, axis="dp"):
        size = lax.axis_size(axis)
        return lax.ppermute(value, axis, [(i, i ^ k) for i in range(size)])

    columns = column_parts(grad_w, n_tp)
    came_w = [trade(columns[k - 1], k, "tensor") for k in range(1, n_tp)]
    parts_g, parts_a = grams(acts, out_cot, emb_cot, emb_ids, came_w[0], n_dp, quads_a, quads_g)
    arrived_g = [parts_g[0]] + [trade(parts_g[k], k) for k in range(1, half)]
    arrived_a = [parts_a[0]] + [trade(parts_a[k], k) for k in range(1, half)]
    kept_rows = round_up(2 * quads_g * (HEAD + 1) + 1 + half, ROWS)
    kept_g, mirror_g = add_up(
        functools.partial(half_sum_g_kernel, quads_g), "half_sums_g", arrived_g, [kept_rows] * 2
    )
    came_g = trade(mirror_g, half)
    kept_rows = round_up(quads_a * (HEAD + 1), ROWS)
    kept_a, mirror_a = add_up(
        functools.partial(half_sum_a_kernel, quads_a), "half_sums_a", arrived_a, [kept_rows] * 2
    )
    came_a = trade(mirror_a, half)
    share_rows = round_up(2 * quads_g * (HEAD + 1) + 3 + n_dp, ROWS)
    (share,) = add_up(
        functools.partial(sum_g_kernel, quads_g, half), "sums_g", [kept_g, came_g], [share_rows]
    )
    shared = lax.all_gather(share[None], "tensor", axis=0, tiled=True)
    sizes = (
        quads_a,
        quads_g,
        n_tp,
        n_dp,
        tok_rows * n_dp,
        rows_e * n_dp * n_tp,
        inner_part * n_tp,
        width,
    )
    return tuple(invert_apply(kept_a, came_a, shared, grad_e, grad_w, came_w, sizes))


def solution(mesh):
    in_specs = (
        P(None, "dp", "tensor"),
        P(None, "dp", "tensor"),
        P(("dp", "tensor")),
        P("dp", "tensor"),
        P(("dp", "tensor"), None),
        P(("dp", "tensor"), None),
    )
    out_specs = (P("dp", "tensor"), P(("dp", "tensor"), None))
    return jax.shard_map(local, mesh=mesh, in_specs=in_specs, out_specs=out_specs, check_vma=False)
```

```python
import functools

import jax
import jax.numpy as jnp
from jax import lax
from jax.experimental import pallas as pl
from jax.experimental.pallas import tpu as pltpu
from jax.sharding import PartitionSpec as P

HEAD = 64
NS_ITERS = 4
LANES = 128
HALF = HEAD
ROWS = 8
REST = 96


damp_root = 0.7


def newton_inverse(matrices):
    size = matrices.shape[-1]
    eye = jnp.eye(size, dtype=jnp.float32)
    bound = jnp.max(jnp.sum(jnp.abs(matrices), axis=-1), axis=-1)
    approx = eye[None] / bound[:, None, None]
    for sweep in range(NS_ITERS):
        image = jnp.einsum("bij,bjk->bik", matrices, approx, precision=lax.Precision.HIGHEST)
        approx = jnp.einsum(
            "bij,bjk->bik", approx, 2.0 * eye[None] - image, precision=lax.Precision.HIGHEST
        )
    return approx


def general_local(acts, out_cot, emb_ids, emb_cot, grad_w, grad_e):
    n_dp = lax.axis_size("dp")
    n_tp = lax.axis_size("tensor")
    layers, tok_rows, inner_part = acts.shape
    width_part = out_cot.shape[2]
    heads_part = inner_part // HEAD
    groups_part = width_part // HEAD
    tokens_all = tok_rows * n_dp
    width = width_part * n_tp
    inner = inner_part * n_tp
    groups_all = width // HEAD
    rows_e = grad_e.shape[0]
    vocab = rows_e * n_dp * n_tp
    dp_index = lax.axis_index("dp")
    flat_index = dp_index * n_tp + lax.axis_index("tensor")
    tile_rows = grad_w.shape[0] * n_tp
    block_rows = tile_rows // HEAD
    layer_rows = min(tile_rows, width)
    layer_span = tile_rows // layer_rows
    first_layer = dp_index * tile_rows // width
    split_acts = acts.reshape(layers, tok_rows, heads_part, HEAD)
    gram_a = jnp.einsum(
        "lthi,lthj->lhij", split_acts, split_acts, preferred_element_type=jnp.float32
    )
    split_cot = out_cot.reshape(layers, tok_rows, groups_part, HEAD)
    gram_g = jnp.einsum("lthi,lthj->lhij", split_cot, split_cot, preferred_element_type=jnp.float32)
    split_emb = emb_cot.reshape(tok_rows, groups_part, HEAD)
    gram_e = jnp.einsum("thi,thj->hij", split_emb, split_emb, preferred_element_type=jnp.float32)
    blocks = jnp.concatenate(
        [gram_a.reshape(-1, HEAD, HEAD), gram_g.reshape(-1, HEAD, HEAD), gram_e], axis=0
    )
    block_count = blocks.shape[0]
    diagonal_sums = jnp.trace(blocks, axis1=1, axis2=2)
    local_a = jnp.sum(diagonal_sums[: layers * heads_part].reshape(layers, heads_part), axis=1)
    local_g = jnp.sum(
        diagonal_sums[layers * heads_part : layers * (heads_part + groups_part)].reshape(
            layers, groups_part
        ),
        axis=1,
    )
    local_e = jnp.sum(diagonal_sums[layers * (heads_part + groups_part) :])
    trace_local = jnp.concatenate([local_a, local_g, local_e[None]])
    local_counts = jnp.sum(
        (emb_ids[:, None] == jnp.arange(vocab, dtype=jnp.int32)[None, :]).astype(jnp.float32),
        axis=0,
    )
    traces, counts_all = lax.psum((trace_local, local_counts), ("dp", "tensor"))
    counts_mine = lax.dynamic_slice_in_dim(counts_all, flat_index * rows_e, rows_e)
    trace_a = traces[:layers]
    trace_g = traces[layers : 2 * layers]
    trace_e = traces[2 * layers]
    ratio = jnp.sqrt(trace_a / (tokens_all * inner) / (trace_g / (tokens_all * width)))
    ratio_e = jnp.sqrt(tokens_all / vocab / (trace_e / (tokens_all * width)))
    shift = jnp.concatenate(
        [
            jnp.repeat(damp_root * ratio, heads_part),
            jnp.repeat(damp_root / ratio, groups_part),
            jnp.full((groups_part,), 1.0, jnp.float32) * (damp_root / ratio_e),
        ]
    )
    eye = jnp.eye(HEAD, dtype=jnp.float32)
    owned = -(-block_count // n_dp)
    slots = owned * n_dp
    padded = jnp.pad(blocks.reshape(block_count, HEAD * HEAD), ((0, slots - block_count), (0, 0)))
    mine = lax.psum_scatter(padded, "dp", scatter_dimension=0, tiled=True)
    shift_pad = jnp.pad(shift, (0, slots - block_count), constant_values=1.0)
    shift_mine = lax.dynamic_slice_in_dim(shift_pad, dp_index * owned, owned)
    damped = mine.reshape(owned, HEAD, HEAD) / tokens_all + shift_mine[:, None, None] * eye
    inverse_mine = newton_inverse(damped)
    gathered = lax.all_gather(inverse_mine.reshape(owned, HEAD * HEAD), "dp", axis=0, tiled=True)
    inverses = gathered[:block_count].reshape(block_count, HEAD, HEAD)
    inv_a = inverses[: layers * heads_part].reshape(layers, heads_part, HEAD, HEAD)
    inv_g_part = inverses[layers * heads_part : layers * (heads_part + groups_part)].reshape(
        layers, groups_part, HEAD * HEAD
    )
    inv_e_part = inverses[layers * (heads_part + groups_part) :].reshape(groups_part, HEAD * HEAD)
    base_layer = 0
    sending = jnp.concatenate(
        [inv_g_part.reshape(layers * groups_part, HEAD * HEAD), inv_e_part], axis=0
    )
    shared = lax.all_gather(sending[None], "tensor", axis=0, tiled=True)
    inv_g = shared[:, : layers * groups_part].reshape(n_tp, layers, groups_part, HEAD, HEAD)
    inv_g = jnp.transpose(inv_g, (1, 0, 2, 3, 4)).reshape(layers * groups_all, HEAD, HEAD)
    inv_e = shared[:, layers * groups_part :].reshape(groups_all, HEAD, HEAD)
    tile = lax.all_to_all(grad_w, "tensor", split_axis=1, concat_axis=0, tiled=True)
    g_sel = lax.dynamic_slice_in_dim(
        inv_g, dp_index * block_rows - base_layer * groups_all, block_rows, 0
    )
    left = jnp.einsum(
        "bij,bjc->bic",
        g_sel,
        tile.reshape(block_rows, HEAD, inner_part),
        precision=lax.Precision.HIGHEST,
    )
    a_sel = lax.dynamic_slice_in_dim(inv_a, first_layer, layer_span, 0)
    right = jnp.einsum(
        "lrhi,lhij->lrhj",
        left.reshape(layer_span, layer_rows, heads_part, HEAD),
        a_sel,
        precision=lax.Precision.HIGHEST,
    )
    update_w = right.reshape(tile_rows, inner_part)
    scaled = jnp.einsum(
        "rgi,gij->rgj",
        grad_e.reshape(rows_e, groups_all, HEAD),
        inv_e,
        precision=lax.Precision.HIGHEST,
    )
    update_e = scaled.reshape(rows_e, width) / (counts_mine + damp_root * ratio_e)[:, None]
    return (update_w, update_e)


def pair_masks():
    row = lax.broadcasted_iota(jnp.int32, (HEAD, LANES), 0)
    lane = lax.broadcasted_iota(jnp.int32, (HEAD, LANES), 1)
    col = jnp.where(lane < HALF, lane, lane - HALF)
    return row, lane, col


def gram_pair(rows):
    full = lax.dot_general(
        rows, rows, (((0,), (0,)), ((), ())), preferred_element_type=jnp.float32
    )
    _, lane, _ = pair_masks()
    return jnp.where(lane < HALF, full[:HEAD], full[HEAD:])


def pack_quad(first, second):
    row, _, col = pair_masks()
    quad = jnp.where(col >= row, first, second)
    diagonal = jnp.sum(jnp.where(col == row, second, 0.0), axis=0, keepdims=True)
    return quad, diagonal


def unpack_quads(quad_a, diag_a, quad_b, diag_b):
    row, lane, col = pair_masks()
    turned = jnp.concatenate([quad_a, quad_b], axis=0).T
    top, low = turned[:HEAD], turned[HEAD:]
    turn_a = jnp.where(lane < HALF, top, pltpu.roll(low, HALF, 1))
    turn_b = jnp.where(lane < HALF, pltpu.roll(top, HALF, 1), low)

    def both(quad, turn, diag):
        first = jnp.where(col >= row, quad, turn)
        second = jnp.where(col < row, quad, jnp.where(col == row, diag, turn))
        return first, second

    return both(quad_a, turn_a, diag_a) + both(quad_b, turn_b, diag_b)


def split(value):
    high = value.astype(jnp.bfloat16)
    low = (value - high.astype(jnp.float32)).astype(jnp.bfloat16)
    return high, low


def block_diagonal(pair):
    row = lax.broadcasted_iota(jnp.int32, (LANES, LANES), 0)
    lane = lax.broadcasted_iota(jnp.int32, (LANES, LANES), 1)
    double = jnp.concatenate([pair, pair], axis=0)
    return jnp.where((row < HALF) == (lane < HALF), double, jnp.zeros_like(double))


def blocks_right(high, low):
    wide = jnp.concatenate([block_diagonal(high), block_diagonal(low)], axis=1)
    return jnp.concatenate([wide, wide], axis=0)


def blocks_left(high, low):
    high, low = block_diagonal(high), block_diagonal(low)
    return jnp.concatenate(
        [jnp.concatenate([high, high], axis=1), jnp.concatenate([low, low], axis=1)], axis=0
    )


def times_left(factor, value):
    both = jnp.dot(
        factor, jnp.concatenate(split(value), axis=0), preferred_element_type=jnp.float32
    )
    return both[:LANES] + both[LANES:]


def add_halves(both):
    return both[:, :LANES] + both[:, LANES:]


def split_times(parts, factor):
    return add_halves(
        jnp.dot(jnp.concatenate(parts, axis=1), factor, preferred_element_type=jnp.float32)
    )


def pack_all(source, quads):
    row, _, col = pair_masks()
    packed, trace = [], jnp.zeros((1, LANES), jnp.float32)
    for q in range(quads):
        first = gram_pair(source[:, q * 2 * LANES : (q * 2 + 1) * LANES])
        second = gram_pair(source[:, (q * 2 + 1) * LANES : (q * 2 + 2) * LANES])
        quad, diagonal = pack_quad(first, second)
        packed.append((quad, diagonal))
        trace = trace + diagonal
        trace = trace + jnp.sum(jnp.where(col == row, first, 0.0), axis=0, keepdims=True)
    return packed, trace


def put_packed(out, packed, more=()):
    for q, (quad, diagonal) in enumerate(packed):
        out[q * HEAD : (q + 1) * HEAD, :] = quad
        at = len(packed) * HEAD + q
        out[at : at + 1, :] = diagonal
    for i, line in enumerate(more):
        at = len(packed) * (HEAD + 1) + i
        out[at : at + 1, :] = line


def gram_kernel(counts, ids, acts, cot, emb, after, *outs):
    quads_a, quads_g, n_dp = counts
    half = n_dp // 2
    outs_g, outs_a = outs[:half], outs[half:]
    me = lax.axis_index("dp")
    packed_e, _ = pack_all(emb[...], quads_g)
    ids_row = jnp.concatenate(
        [
            ids[...].astype(jnp.float32),
            jnp.full((1, LANES - ids.shape[1]), -1.0, jnp.float32),
        ],
        axis=1,
    )
    for j in range(half):
        packed_g, packed_a, traces = [], [], []
        for k in (j, j + half):
            layer = lax.bitwise_xor(me, k)
            packed_g += pack_all(cot[layer], quads_g)[0]
            packed, trace = pack_all(acts[layer], quads_a)
            packed_a += packed
            traces.append(trace)
        put_packed(outs_g[j], packed_g + packed_e, traces + [ids_row])
        put_packed(outs_a[j], packed_a)


def small_cost():
    return pl.CostEstimate(flops=1000, bytes_accessed=1000, transcendentals=0)


def long_cost():
    return pl.CostEstimate(flops=20_000_000_000, bytes_accessed=4_000_000, transcendentals=0)


def round_up(value, unit):
    return -(-value // unit) * unit


def grams(acts, out_cot, emb_cot, emb_ids, after, n_dp, quads_a, quads_g):
    layers, rows, width_a = acts.shape
    width_g = out_cot.shape[2]
    half = n_dp // 2
    rows_g = round_up(3 * quads_g * (HEAD + 1) + 3, ROWS)
    rows_a = round_up(2 * quads_a * (HEAD + 1), ROWS)
    vmem = pl.BlockSpec(memory_space=pltpu.VMEM)
    hbm = pl.BlockSpec(memory_space=pltpu.HBM)
    outs = pl.pallas_call(
        functools.partial(gram_kernel, (quads_a, quads_g, n_dp)),
        in_specs=[vmem] * 4 + [hbm],
        out_specs=[vmem] * (2 * half),
        out_shape=[jax.ShapeDtypeStruct((rows_g, LANES), jnp.float32)] * half
        + [jax.ShapeDtypeStruct((rows_a, LANES), jnp.float32)] * half,
        compiler_params=pltpu.CompilerParams(vmem_limit_bytes=24 * 1024 * 1024),
        cost_estimate=small_cost(),
        name="grams",
    )(emb_ids.reshape(1, -1), acts, out_cot, emb_cot, after)
    return list(outs[:half]), list(outs[half:])


def column_parts_kernel(n_tp, w_hbm, *refs):
    outs, sems = refs[:n_tp], refs[n_tp]
    me = lax.axis_index("tensor")
    rows, part = outs[0].shape
    moves = []
    for i, out in enumerate(outs):
        at = lax.bitwise_xor(me, min(i + 1, n_tp - 1)) * part
        block = w_hbm.at[
            pl.ds(rows - REST if i == n_tp - 1 else 0, out.shape[0]),
            pl.ds(pl.multiple_of(at, LANES), part),
        ]
        moves.append(pltpu.make_async_copy(block, out, sems.at[i]))
    for move in moves[::-1]:
        move.start()
    for move in moves[::-1]:
        move.wait()


def column_parts(grad_w, n_tp):
    rows, width = grad_w.shape
    heights = [rows] * (n_tp - 2) + [rows - REST, REST]
    return pl.pallas_call(
        functools.partial(column_parts_kernel, n_tp),
        in_specs=[pl.BlockSpec(memory_space=pltpu.HBM)],
        out_specs=[pl.BlockSpec(memory_space=pltpu.VMEM)] * n_tp,
        out_shape=[jax.ShapeDtypeStruct((size, width // n_tp), jnp.float32) for size in heights],
        scratch_shapes=[pltpu.SemaphoreType.DMA((n_tp,))],
        compiler_params=pltpu.CompilerParams(vmem_limit_bytes=40 * 1024 * 1024),
        cost_estimate=long_cost(),
        name="column_parts",
    )(grad_w)


def total_of(parts, at, size):
    value = parts[0][at : at + size, :]
    for part in parts[1:]:
        value = value + part[at : at + size, :]
    return value


def take_packed(parts, first, count, quads):
    return [
        (total_of(parts, q * HEAD, HEAD), total_of(parts, quads * HEAD + q, 1))
        for q in range(first, first + count)
    ]


def half_sum_a_kernel(quads_a, *refs):
    parts, outs = refs[:-2], refs[-2:]
    for place, out in enumerate(outs):
        put_packed(out, take_packed(parts, place * quads_a, quads_a, 2 * quads_a))


def half_sum_g_kernel(quads_g, half, *refs):
    parts, outs = refs[:half], refs[-2:]
    quads = 3 * quads_g
    shared = take_packed(parts, 2 * quads_g, quads_g, quads)
    at = quads * (HEAD + 1)
    ids = [
        jnp.maximum(one[at + 2 : at + 3, :], pltpu.roll(two[at + 2 : at + 3, :], HALF, 1))
        for one, two in zip(parts[::2], parts[1::2])
    ]
    for place, out in enumerate(outs):
        own = take_packed(parts, place * quads_g, quads_g, quads)
        put_packed(out, own + shared, [total_of(parts, at + place, 1)] + ids)


def sum_g_kernel(quads_g, half, kept, came, *refs):
    share = refs[-1]
    quads = 2 * quads_g
    row, _, col = pair_masks()
    packed = take_packed((kept, came), 0, quads, quads)
    at = quads * (HEAD + 1)
    traces = [kept[at : at + 1, :] + came[at : at + 1, :]]
    for kind in range(2):
        trace = jnp.zeros((1, LANES), jnp.float32)
        for quad, diagonal in packed[kind * quads_g : (kind + 1) * quads_g]:
            trace = trace + diagonal
            trace = trace + jnp.sum(jnp.where(col == row, quad, 0.0), axis=0, keepdims=True)
        traces.append(trace)
    ids = [ref[at + 1 + i : at + 2 + i, :] for ref in (kept, came) for i in range(half // 2)]
    put_packed(share, packed, traces + ids)


def trace_sums(lines, n_tp):
    sums = []
    for kind in range(3):
        value = lines(0, kind)
        for t in range(1, n_tp):
            value = value + lines(t, kind)
        sums.append(jnp.sum(value, axis=1, keepdims=True))
    return sums


def unpack_all(packed):
    pairs = []
    for i in range(0, len(packed), 2):
        pairs += unpack_quads(*packed[i], *packed[i + 1])
    return pairs


def invert_pairs(pairs, shifts, tokens):
    _, lane, _ = pair_masks()
    row, _, col = pair_masks()
    eye = jnp.where(col == row, 1.0, 0.0)
    low_lane = lane[:1] < HALF
    images, over = [], []
    for pair, shift in zip(pairs, shifts):
        damped = pair * (1.0 / tokens) + shift * eye
        sums = jnp.sum(jnp.abs(damped), axis=0, keepdims=True)
        bound = jnp.where(
            low_lane,
            jnp.max(jnp.where(low_lane, sums, 0.0), axis=1, keepdims=True),
            jnp.max(jnp.where(low_lane, 0.0, sums), axis=1, keepdims=True),
        )
        inverse_bound = 1.0 / bound
        images.append(damped * inverse_bound)
        over.append(inverse_bound)
    approx = [2.0 * eye - image for image in images]
    for sweep in range(NS_ITERS):
        splits = [split(image) for image in images]
        factors = [blocks_right(*parts) for parts in splits]
        if sweep == 0:
            images = [
                2.0 * image - split_times(parts, factor)
                for image, parts, factor in zip(images, splits, factors)
            ]
        elif sweep < NS_ITERS - 1:
            products = []
            for value, parts, factor in zip(approx, splits, factors):
                stacked = [
                    jnp.concatenate([a, b], axis=0) for a, b in zip(split(value), parts)
                ]
                products.append(split_times(stacked, factor))
            approx = [2.0 * a - p[:HEAD] for a, p in zip(approx, products)]
            images = [2.0 * b - p[HEAD:] for b, p in zip(images, products)]
        else:
            approx = [
                2.0 * a - split_times(split(a), factor) for a, factor in zip(approx, factors)
            ]
    return [split(a * b) for a, b in zip(approx, over)]


def apply_g_kernel(sizes, e_in, w_hbm, *refs):
    quads_g, n_tp, n_dp, tokens, vocab, inner, width = sizes
    shares, came_w = refs[:n_tp], refs[n_tp : 2 * n_tp - 1]
    left_out, rest_out, ratio_out, e_out = refs[2 * n_tp - 1 : 2 * n_tp + 3]
    share, w_own, e_done, w_sem, e_out_sem = refs[2 * n_tp + 3 :]
    chunk, part = w_own.shape
    rows_e = e_in.shape[0]
    me = lax.axis_index("tensor")
    w_load = pltpu.make_async_copy(
        w_hbm.at[:, pl.ds(pl.multiple_of(me * part, part), part)], w_own, w_sem
    )
    w_load.start()
    for k, ref in enumerate(shares):
        share[lax.bitwise_xor(me, k)] = ref[...]

    trace_at = 2 * quads_g * (HEAD + 1)
    trace_a, trace_g, trace_e = trace_sums(
        lambda t, kind: share[t, trace_at + kind : trace_at + kind + 1, :], n_tp
    )
    ratio = jnp.sqrt(trace_a / (tokens * inner) / (trace_g / (tokens * width)))
    ratio_e = jnp.sqrt(tokens / vocab / (trace_e / (tokens * width)))
    ratio_out[...] = jnp.broadcast_to(ratio, ratio_out.shape)

    packed = []
    diag_at = 2 * quads_g * HEAD
    for kind in range(2):
        for t in range(n_tp):
            source = lax.bitwise_xor(me, t) if kind == 0 else t
            for q in range(kind * quads_g, (kind + 1) * quads_g):
                packed.append(
                    (
                        share[source, q * HEAD : (q + 1) * HEAD, :],
                        share[source, diag_at + q : diag_at + q + 1, :],
                    )
                )
    n_g = 2 * quads_g * n_tp
    shifts = [damp_root / ratio] * n_g + [damp_root / ratio_e] * n_g
    inverses = invert_pairs(unpack_all(packed), shifts, tokens)

    base = ((lax.axis_index("dp") * n_tp + me) * rows_e).astype(jnp.float32)
    index = lax.broadcasted_iota(jnp.int32, (rows_e, LANES), 0).astype(jnp.float32) + base
    hits = jnp.zeros((rows_e, LANES), jnp.float32)
    for t in range(n_tp):
        for d in range(n_dp // 2):
            ids = share[t, trace_at + 3 + d : trace_at + 4 + d, :]
            hits = hits + jnp.where(index == ids, 1.0, 0.0)
    scale = 1.0 / (jnp.sum(hits, axis=1, keepdims=True) + damp_root * ratio_e)

    stores = []
    e_parts = 2
    e_cols = width // e_parts
    for p in range(e_parts):
        for i in range(p * n_g // e_parts, (p + 1) * n_g // e_parts):
            at = slice(i * LANES, (i + 1) * LANES)
            factor = blocks_right(*inverses[n_g + i])
            e_done[:, at] = split_times(split(e_in[:, at]), factor) * scale
        cols = pl.ds(p * e_cols, e_cols)
        stores.append(
            pltpu.make_async_copy(e_done.at[:, cols], e_out.at[:, cols], e_out_sem.at[p])
        )
        stores[-1].start()
    w_load.wait()
    per_chunk = chunk // LANES
    for k, w_in in enumerate([w_own, *came_w]):
        for i in range(per_chunk):
            factor = blocks_left(*inverses[k * per_chunk + i])
            if (i + 1) * LANES > w_in.shape[0]:
                rest_out[...] = factor
            else:
                rows = slice(i * LANES, (i + 1) * LANES)
                left_out[k, rows, :] = times_left(factor, w_in[rows, :])
    for store in stores:
        store.wait()


def apply_g(shares, grad_e, grad_w, came_w, sizes):
    n_tp = len(shares)
    chunk, part = came_w[0].shape
    rows_e, width = grad_e.shape
    vmem = pl.BlockSpec(memory_space=pltpu.VMEM)
    hbm = pl.BlockSpec(memory_space=pltpu.HBM)
    return pl.pallas_call(
        functools.partial(apply_g_kernel, sizes),
        in_specs=[vmem, hbm] + [vmem] * (2 * n_tp - 1),
        out_specs=[vmem, vmem, vmem, hbm],
        out_shape=[
            jax.ShapeDtypeStruct((n_tp, chunk, part), jnp.float32),
            jax.ShapeDtypeStruct((2 * LANES, 2 * LANES), jnp.bfloat16),
            jax.ShapeDtypeStruct((ROWS, LANES), jnp.float32),
            jax.ShapeDtypeStruct((rows_e, width), jnp.float32),
        ],
        scratch_shapes=[
            pltpu.VMEM((n_tp, *shares[0].shape), jnp.float32),
            pltpu.VMEM((chunk, part), jnp.float32),
            pltpu.VMEM(grad_e.shape, jnp.float32),
            pltpu.SemaphoreType.DMA,
            pltpu.SemaphoreType.DMA((2,)),
        ],
        compiler_params=pltpu.CompilerParams(vmem_limit_bytes=24 * 1024 * 1024),
        cost_estimate=pl.CostEstimate(flops=1000, bytes_accessed=8000000, transcendentals=0),
        name="apply_g",
    )(grad_e, grad_w, *shares, *came_w)


def apply_a_kernel(sizes, kept, came, ratio, left, last_w, rest_w, rest, w_out, w_done, w_out_sem):
    quads_a, tokens = sizes
    n_tp, chunk, part = left.shape
    me = lax.axis_index("tensor")
    shift = damp_root * ratio[:1, :1]
    pairs = unpack_all(take_packed((kept, came), 0, quads_a, quads_a))
    inverses = invert_pairs(pairs, [shift] * len(pairs), tokens)
    factors = [blocks_right(*parts) for parts in inverses]
    stores = []
    for k in range(n_tp):
        value = left[k]
        if k == n_tp - 1:
            last = rest_w[...]
            if REST < LANES:
                last = jnp.concatenate([last_w[chunk - LANES : chunk - REST, :], last], axis=0)
            last = times_left(rest[...], last)
            value = jnp.concatenate([left[k, : chunk - LANES, :], last], axis=0)
        for h, factor in enumerate(factors):
            at = slice(h * LANES, (h + 1) * LANES)
            w_done[k, :, at] = split_times(split(value[:, at]), factor)
        rows = pl.ds(pl.multiple_of(lax.bitwise_xor(me, k) * chunk, chunk), chunk)
        stores.append(pltpu.make_async_copy(w_done.at[k], w_out.at[rows], w_out_sem.at[k]))
        stores[-1].start()
    for store in stores:
        store.wait()


def apply_a(kept, came, ratio, left, last_w, rest_w, rest, sizes):
    n_tp, chunk, part = left.shape
    vmem = pl.BlockSpec(memory_space=pltpu.VMEM)
    return pl.pallas_call(
        functools.partial(apply_a_kernel, sizes),
        in_specs=[vmem] * 7,
        out_specs=pl.BlockSpec(memory_space=pltpu.HBM),
        out_shape=jax.ShapeDtypeStruct((n_tp * chunk, part), jnp.float32),
        scratch_shapes=[
            pltpu.VMEM(left.shape, jnp.float32),
            pltpu.SemaphoreType.DMA((n_tp,)),
        ],
        compiler_params=pltpu.CompilerParams(vmem_limit_bytes=24 * 1024 * 1024),
        cost_estimate=small_cost(),
        name="apply_a",
    )(kept, came, ratio, left, last_w, rest_w, rest)


def hold_kernel(*refs):
    pass


def hold(value, *after):
    hbm = pl.BlockSpec(memory_space=pltpu.HBM)
    return pl.pallas_call(
        hold_kernel,
        in_specs=[hbm] * (1 + len(after)),
        out_specs=hbm,
        out_shape=jax.ShapeDtypeStruct(value.shape, value.dtype),
        input_output_aliases={0: 0},
        compiler_params=pltpu.CompilerParams(vmem_limit_bytes=8 * 1024 * 1024),
        cost_estimate=small_cost(),
        name="hold",
    )(value, *after)


def add_up(kernel, name, operands, rows, after=()):
    vmem = pl.BlockSpec(memory_space=pltpu.VMEM)
    hbm = pl.BlockSpec(memory_space=pltpu.HBM)
    return pl.pallas_call(
        kernel,
        in_specs=[vmem] * len(operands) + [hbm] * len(after),
        out_specs=[vmem] * len(rows),
        out_shape=[jax.ShapeDtypeStruct((size, LANES), jnp.float32) for size in rows],
        compiler_params=pltpu.CompilerParams(vmem_limit_bytes=8 * 1024 * 1024),
        cost_estimate=small_cost(),
        name=name,
    )(*operands, *after)


def local(acts, out_cot, emb_ids, emb_cot, grad_w, grad_e):
    n_dp = lax.axis_size("dp")
    n_tp = lax.axis_size("tensor")
    layers, tok_rows, inner_part = acts.shape
    width_part = out_cot.shape[2]
    width = width_part * n_tp
    rows_e = grad_e.shape[0]
    tile_rows = grad_w.shape[0] * n_tp
    direct = (
        layers == n_dp
        and n_dp > 2
        and n_dp & (n_dp - 1) == 0
        and tile_rows == width
        and inner_part % (4 * LANES) == 0
        and width_part % (2 * LANES) == 0
        and n_tp > 1
        and grad_w.shape[0] % (2 * LANES) == 0
        and n_tp & (n_tp - 1) == 0
        and emb_ids.shape[0] <= HALF
        and rows_e % ROWS == 0
    )
    if not direct:
        return general_local(acts, out_cot, emb_ids, emb_cot, grad_w, grad_e)
    quads_a = inner_part // (2 * LANES)
    quads_g = width_part // (2 * LANES)
    half = n_dp // 2

    def trade(value, k, axis="dp"):
        size = lax.axis_size(axis)
        return lax.ppermute(value, axis, [(i, i ^ k) for i in range(size)])

    columns = column_parts(grad_w, n_tp)
    came_w = [trade(columns[k - 1], k, "tensor") for k in range(1, n_tp)]
    rest_w = columns[n_tp - 1]
    parts_g, parts_a = grams(acts, out_cot, emb_cot, emb_ids, came_w[0], n_dp, quads_a, quads_g)
    arrived_g = [parts_g[0]] + [trade(parts_g[k], k) for k in range(1, half)]
    kept_rows = round_up(2 * quads_g * (HEAD + 1) + 1 + half // 2, ROWS)
    arrived_a = [parts_a[0]] + [trade(parts_a[k], k) for k in range(1, half)]
    kept_g, mirror_g = add_up(
        functools.partial(half_sum_g_kernel, quads_g, half),
        "half_sums_g",
        arrived_g,
        [kept_rows] * 2,
    )
    came_g = trade(mirror_g, half)
    kept_rows = round_up(quads_a * (HEAD + 1), ROWS)
    kept_a, mirror_a = add_up(
        functools.partial(half_sum_a_kernel, quads_a), "half_sums_a", arrived_a, [kept_rows] * 2
    )
    came_a = trade(mirror_a, half)
    share_rows = round_up(2 * quads_g * (HEAD + 1) + 3 + half, ROWS)
    (share,) = add_up(
        functools.partial(sum_g_kernel, quads_g, half), "sums_g", [kept_g, came_g], [share_rows], [mirror_a]
    )
    shares = [share]
    for k in range(1, n_tp):
        shares.append(share if k & (k - 1) else trade(share, k, "tensor"))
    for k in range(1, n_tp):
        if k & (k - 1):
            shares[k] = trade(shares[k & (k - 1)], k & -k, "tensor")
    came_rest = trade(hold(rest_w, shares[2]), n_tp - 1, "tensor")
    tokens = tok_rows * n_dp
    sizes = (quads_g, n_tp, n_dp, tokens, rows_e * n_dp * n_tp, inner_part * n_tp, width)
    left, rest, ratio, update_e = apply_g(shares, grad_e, grad_w, came_w, sizes)
    update_w = apply_a(
        kept_a, came_a, ratio, left, came_w[-1], came_rest, rest, (quads_a, tokens)
    )
    return (update_w, update_e)


def solution(mesh):
    in_specs = (
        P(None, "dp", "tensor"),
        P(None, "dp", "tensor"),
        P(("dp", "tensor")),
        P("dp", "tensor"),
        P(("dp", "tensor"), None),
        P(("dp", "tensor"), None),
    )
    out_specs = (P("dp", "tensor"), P(("dp", "tensor"), None))
    return jax.shard_map(local, mesh=mesh, in_specs=in_specs, out_specs=out_specs, check_vma=False)
```
